256 devices in a mesh: blk: 32 (over z, x), rep: 8 (over y, core).
Axes of the slice: x: 4, y: 4, z: 8, core: 2. Of those that a mesh axis runs over, the one named last changes fastest.
Arguments:
- features: bfloat16 [131072, 256], P(('blk', 'rep')), may hold values from -6 to 6
- weight: bfloat16 [256, 256], replicated, may hold values from -0.375 to 0.375
- tiles: bfloat16 [256, 32, 2, 128, 128], P(('blk', 'rep')), may hold values from -0.1875 to 0.1875
- tile_place: int32 [256, 32, 2], P(('blk', 'rep')), may hold values from 0 to 127
- tile_count: int32 [256, 32], P(('blk', 'rep')), may hold values from 1 to 2, as said below
- cotangent: bfloat16 [131072, 256], P(('blk', 'rep')), may hold values from -6 to 6
Outputs:
- output: bfloat16 [131072, 256], P(('blk', 'rep'))
- grad_features: bfloat16 [131072, 256], P(('blk', 'rep'))
- grad_weight: float32 [256, 256], replicated
The draws below stay inside these ranges and needn't reach their ends.
Inputs may be any that keep to these rules, and one draw needn't show every extreme that they name: Slots at or beyond tile_count of a device and offset hold no part of the adjacency; one device fills all 2 slots for every offset.
All inputs are finite; a program needn't handle non-finite values.
Results may differ from the reference program's by a relative error of at most 0.018.
Values may be sent and summed in bfloat16 or wider, within the bound.
A program may use at most 128 MiB of HBM per device.

```python
import math
import jax
import jax.numpy as jnp
from jax import lax

FIN = 256
FOUT = 256
BS = 128
SLOTS = 2
NODES = 131072
TB = 32
CB = 4
N_BLK = 32
N_REP = 8


def draw_tile_count(key, part):
    key = jax.random.fold_in(key, 11)
    keys = jax.random.split(key, 3)
    dev_total = N_BLK * N_REP
    level = jax.random.randint(keys[0], (dev_total, 1), 2, SLOTS + 1)
    lowest = (level + 1) // 2
    spread = jax.random.randint(keys[1], (dev_total, N_BLK), 0, SLOTS + 1)
    counts = lowest + spread % (level - lowest + 1)
    busiest = jax.random.randint(keys[2], (), 0, dev_total)
    dev_rows = jnp.arange(dev_total)[:, None]
    return jnp.where(dev_rows == busiest, SLOTS, counts).astype(jnp.int32)


def set_ends(result, stream_key, low, top_value):
    shape = result.shape
    place = [jax.random.randint(jax.random.fold_in(stream_key, axis), (), 0, shape[axis]) for axis in range(len(shape))]
    result = result.at[tuple(place)].set(low)
    longest = shape.index(max(shape))
    place[longest] = (place[longest] + 1) % shape[longest]
    return result.at[tuple(place)].set(top_value)


def block_scale(key, dims, shards, least, top_value):
    gain = 1.0
    for axis_at, shards_of in shards:
        steps = jax.random.uniform(jax.random.fold_in(jax.random.fold_in(key, 6), axis_at), (shards_of,), jnp.float32, least / len(shards), top_value / len(shards))
        gain = gain * jnp.repeat(jnp.exp(steps), dims[axis_at] // shards_of).reshape((-1,) + (1,) * (len(dims) - 1 - axis_at))
    return gain


def scatter_about(own_key, extent, deviation, bound, shards=(), kind=jnp.bfloat16):
    values = deviation * jax.random.normal(own_key, extent, jnp.float32)
    if shards:
        values = values * block_scale(own_key, extent, shards, -0.22, 0.18)
    return jnp.clip(values, -bound, bound).astype(kind)


def setup_inputs(seed: int = 0) -> dict:
    key_of = jax.random.split(jax.random.key(seed), 7)
    return {
        "features": scatter_about(key_of[0], (NODES, FIN), 1.0, 6.0, ((0, 256),)),
        "weight": scatter_about(key_of[1], (FIN, FOUT), FIN ** -0.5, 0.375),
        "tiles": scatter_about(key_of[2], (N_BLK * N_REP, N_BLK, SLOTS, BS, BS), (BS * N_BLK * N_REP * SLOTS // (2 * TB)) ** -0.5, 0.1875, ((0, 256),)),
        "tile_place": set_ends(jax.random.randint(key_of[3], (N_BLK * N_REP, N_BLK, SLOTS), 0, TB * CB), jax.random.fold_in(key_of[3], 1), 0, (TB * CB) - 1).astype(jnp.int32),
        "tile_count": draw_tile_count(jax.random.fold_in(key_of[6], 71), 0),
        "cotangent": scatter_about(key_of[5], (NODES, FOUT), 1.0, 6.0, ((0, 256),)),
    }


def block_spots(dev_id, tile_place, tile_count):
    team_id = dev_id // N_REP
    share_id = dev_id % N_REP
    offsets = jnp.arange(N_BLK).astype(jnp.int32)
    col_team = (team_id - offsets) % N_BLK
    places = tile_place[dev_id]
    row_block = team_id * TB + places // CB
    col_block = (col_team[:, None] * N_REP + share_id) * CB + places % CB
    live = jnp.arange(SLOTS)[None, :] < tile_count[dev_id][:, None]
    return (row_block.astype(jnp.int32), col_block.astype(jnp.int32), live)

def reference(features, weight, tiles, tile_place, tile_count, cotangent):
    feat_blocks = features.reshape(NODES // BS, BS, FIN)

    def forward_dev(dev_id, acc):
        row_block, col_block, live = block_spots(dev_id, tile_place, tile_count)
        source = feat_blocks[col_block].astype(jnp.float32)
        dense = tiles[dev_id].astype(jnp.float32) * live[:, :, None, None].astype(jnp.float32)
        product = jnp.einsum('oskj,osjf->oskf', dense, source, precision=lax.Precision.HIGHEST)
        return acc.at[row_block].add(product)
    summed = lax.fori_loop(0, N_BLK * N_REP, forward_dev, jnp.zeros((NODES // BS, BS, FIN), jnp.float32))
    aggregated = summed.reshape(NODES, FIN).astype(jnp.bfloat16)
    pre = jnp.dot(aggregated, weight, preferred_element_type=jnp.float32)
    output = jax.nn.silu(pre).astype(jnp.bfloat16)
    gate = jax.nn.sigmoid(pre)
    grad_pre = (cotangent.astype(jnp.float32) * gate * (1.0 + pre * (1.0 - gate))).astype(jnp.bfloat16)
    grad_weight = jnp.dot(aggregated.T, grad_pre, preferred_element_type=jnp.float32) / math.sqrt(NODES)
    grad_mixed = jnp.dot(grad_pre, weight.T, preferred_element_type=jnp.float32).astype(jnp.bfloat16)
    grad_blocks = grad_mixed.reshape(NODES // BS, BS, FIN)

    def backward_dev(dev_id, acc):
        row_block, col_block, live = block_spots(dev_id, tile_place, tile_count)
        source = grad_blocks[row_block].astype(jnp.float32)
        dense = tiles[dev_id].astype(jnp.float32) * live[:, :, None, None].astype(jnp.float32)
        product = jnp.einsum('oskj,oskf->osjf', dense, source, precision=lax.Precision.HIGHEST)
        return acc.at[col_block].add(product)
    back = lax.fori_loop(0, N_BLK * N_REP, backward_dev, jnp.zeros((NODES // BS, BS, FIN), jnp.float32))
    grad_features = back.reshape(NODES, FIN).astype(jnp.bfloat16)
    return (output, grad_features, grad_weight)
```

```python
import functools
import math

import jax
import jax.numpy as jnp
from jax import lax
from jax.experimental import pallas as pl
from jax.experimental.pallas import tpu as pltpu
from jax.sharding import PartitionSpec as P

NZ, NX, NY, NC = 8, 4, 4, 2
BS = 128
F32, BF16 = jnp.float32, jnp.bfloat16
SEM_TOTAL = 220


def rem(a, n):
    return lax.rem(a, jnp.int32(n))


def kernel(
    feat_ref, weight_ref, tiles_ref, code_ref, cot_ref,
    out_ref, gfeat_ref, gweight_ref,
    feats, held0, held1, held2, held3, passing, meta, meta_s, sums, part, sib,
    land_big1, land_big2, land_small1, land_small2,
    agg, grad0, grad1, turned, lhs, rhs, terms, z_out, z_in,
    w_mine, w_z, w_x, w_y, w_c, w_all,
    send_sem, recv_sem, local_sem, meta_sem,
):
    blk, rep = lax.axis_index("blk"), lax.axis_index("rep")
    z, x = lax.div(blk, jnp.int32(NX)), rem(blk, NX)
    y, core = lax.div(rep, jnp.int32(NC)), rem(rep, NC)

    held, grad = (held0, held1, held2, held3), (grad0, grad1)

    def dev(dz=0, dx=0, dy=0, dc=0):
        return {
            "blk": rem(z + dz + NZ, NZ) * NX + rem(x + dx + NX, NX),
            "rep": rem(y + dy + NY, NY) * NC + rem(core + dc, NC),
        }

    peers = [dev(dc=1)]
    peers += [dev(dx=d) for d in range(1, NX)]
    peers += [dev(dy=d) for d in range(1, NY)]
    peers += [dev(dz=d) for d in range(1, NZ)]
    started = []

    def send(src, dst, target):
        n = len(started)
        copy = pltpu.make_async_remote_copy(
            src_ref=src, dst_ref=dst, send_sem=send_sem.at[n], recv_sem=recv_sem.at[n],
            device_id=target, device_id_type=pl.DeviceIdType.MESH,
        )
        copy.start()
        started.append(copy)
        return copy

    own_tiles = pltpu.make_async_copy(tiles_ref.at[:, 0], held[0], local_sem)
    own_tiles.start()

    barrier = pltpu.get_barrier_semaphore()
    for peer in peers:
        pl.semaphore_signal(barrier, inc=1, device_id=peer, device_id_type=pl.DeviceIdType.MESH)

    for q in range(4):
        feats[0, q] = feat_ref[q * BS:(q + 1) * BS, :]

    pl.semaphore_wait(barrier, len(peers))

    gather_r = [send(feats.at[0], feats.at[1], dev(dz=1))]
    gather_l = [send(feats.at[0], feats.at[7], dev(dz=-1))]
    tile_a = send(tiles_ref.at[0:4, 2], passing.at[0], dev(dx=1))
    tile_b = send(tiles_ref.at[4:8, 2], passing.at[1], dev(dx=-1))

    code = code_ref[...]
    ids = lax.broadcasted_iota(jnp.int32, (BS, BS), 0)
    lanes = lax.broadcasted_iota(jnp.int32, (BS, BS), 1)
    flipped = code.T

    def parts_of(value, at):
        inside = at < 64
        live = jnp.logical_and(value >= 128, inside)
        group = jnp.where(inside, (at >> 1) & 3, -1)
        row = jnp.where(live, (value & 127) >> 2, 32)
        return live, group, row, value & 3

    live_e, group_e, row_e, col_e = parts_of(code, ids)
    live_f, group_f, row_f, col_f = parts_of(flipped, lanes)
    key_e, key_f = row_e * 64 + ids, row_f * 64 + lanes
    before = jnp.logical_and(jnp.logical_and(group_e == group_f, lanes < 64), key_f < key_e)

    def count(flags, axis):
        return jnp.sum(jnp.where(flags, 1, 0), axis=axis, keepdims=True)

    rank = count(before, 1)
    same = count(jnp.logical_and(before, row_e == row_f), 1)
    chosen = jnp.logical_and(
        jnp.logical_and(group_e == (lanes >> 4), ids < 64), rank == (lanes & 15)
    )
    entry = (ids >> 3) * 2 + (ids & 1)
    meta[0, 0:1, :] = jnp.sum(jnp.where(chosen, entry, 0), axis=0, keepdims=True)
    meta[0, 1:2, :] = jnp.sum(jnp.where(chosen, col_e, 0), axis=0, keepdims=True)
    meta[0, 2:3, :] = count(jnp.logical_and(chosen, same == 0), 0)
    mine = jnp.logical_and(live_e, group_e == (lanes >> 5))
    here = count(jnp.logical_and(mine, row_e == (lanes & 31)), 0)
    upto = count(jnp.logical_and(mine, row_e <= (lanes & 31)), 0)
    meta[0, 3:4, :] = jnp.where(here > 0, upto - 1, 16)
    meta[0, 4:5, :] = jnp.where(live_f, row_f, 0)[0:1, :]
    meta[0, 5:6, :] = jnp.where(live_f, col_f, 4)[0:1, :]
    meta[0, 6:8, :] = jnp.zeros((2, BS), jnp.int32)
    meta_copies = [send(meta.at[0], meta.at[k], dev(dx=-k)) for k in (1, 2, 3)]
    sums[16] = jnp.zeros((BS, 2 * BS), F32)

    gather_r[0].wait_recv()
    gather_r.append(send(feats.at[1], feats.at[2], dev(dz=1)))
    gather_l[0].wait_recv()
    gather_l.append(send(feats.at[7], feats.at[6], dev(dz=-1)))
    tile_a.wait_recv()
    tile_fa = send(passing.at[0], held[2].at[0:4], dev(dx=1))
    tile_b.wait_recv()
    tile_fb = send(passing.at[1], held[2].at[4:8], dev(dx=-1))
    tile_1 = send(tiles_ref.at[:, 1], held[1], dev(dx=-1))
    tile_3 = send(tiles_ref.at[:, 3], held[3], dev(dx=1))
    gather_r[1].wait_recv()
    gather_r.append(send(feats.at[2], feats.at[3], dev(dz=1)))
    gather_l[1].wait_recv()
    gather_l.append(send(feats.at[6], feats.at[5], dev(dz=-1)))
    for copy in meta_copies:
        copy.wait_recv()
    to_s = pltpu.make_async_copy(meta, meta_s, meta_sem)
    to_s.start()
    gather_r[2].wait_recv()
    half_r = send(feats.at[3, 0:2], feats.at[4, 0:2], dev(dz=1))
    gather_l[2].wait_recv()
    half_l = send(feats.at[5, 2:4], feats.at[4, 2:4], dev(dz=-1))
    to_s.wait()
    own_tiles.wait()
    half_r.wait_recv()
    half_l.wait_recv()

    sib_copies = {}

    def forward(k):
        carry = lax.div(x + k, jnp.int32(NX))

        def four(g, total):
            for u in range(4):
                at = k * 16 + g * 4 + u
                e, col, fresh = meta_s[k, 0, at] & 15, meta_s[k, 1, at] & 3, meta_s[k, 2, at]
                product = jnp.dot(
                    held[k][e >> 1, e & 1], feats[((e >> 1) + carry) & 7, col], preferred_element_type=F32
                )
                total = product + total * (1 - fresh).astype(F32)
                sums[g * 4 + u] = total
            return total

        lax.fori_loop(0, 4, four, jnp.zeros((BS, 2 * BS), F32))

        def place(i, _):
            for cc in range(2):
                for q in range(4):
                    row = (i * 2 + cc) * 4 + q
                    value = sums[jnp.clip(meta_s[k, 3, k * 32 + row], 0, 16)].astype(BF16)
                    part[0, k, i, cc, q] = value[:, :BS]
                    part[1, k, i, cc, q] = value[:, BS:]
            return 0

        lax.fori_loop(0, 4, place, 0)
        for c in range(2):
            sib_copies[c, k] = send(part.at[c, k, :, 1 - core], sib.at[c, k], dev(dc=1))

    forward(0)
    tile_fa.wait_recv()
    tile_fb.wait_recv()
    forward(2)
    tile_1.wait_recv()
    forward(1)
    tile_3.wait_recv()
    forward(3)

    def add(ref, index, *others):
        value = ref[index].astype(F32)
        for other, at in others:
            value = value + other[at].astype(F32)
        return value

    def merge(c, k):
        sib_copies[c, k].wait_recv()

        def one(i, _):
            for q in range(4):
                part[c, k, i, core, q] = add(part, (c, k, i, core, q), (sib, (c, k, i, q))).astype(BF16)
            return 0

        lax.fori_loop(0, NY, one, 0)

    def near(value, step, size):
        return rem(value + step + size, size)

    class Reduce:
        def __init__(self, c, half):
            self.c, self.half = c, half
            self.n = c * 2 + half

        def step(self, d):
            return dev(dx=d) if self.half == 0 else dev(dy=d)

        def cross(self, d):
            return dev(dy=d) if self.half == 0 else dev(dx=d)

        def big(self, away, lo, size):
            q = pl.ds(2 * self.half, 2)
            if self.half == 0:
                return (self.c, away & 3, pl.ds(lo, size), core, q)
            return (self.c, pl.ds(lo, size), near(y, away, NY), core, q)

        def big_block(self, away, at, q):
            if self.half == 0:
                return (self.c, away & 3, at, core, q)
            return (self.c, at, near(y, away, NY), core, 2 + q)

        def small(self, away, q):
            if self.half == 0:
                return (self.c, 0, near(y, away, NY), core, q)
            return (self.c, away & 3, y, core, 2 + q)

        def begin(self):
            n = self.n
            self.r1 = send(part.at[self.big(2, 0, 2)], land_big1.at[n, 0], self.step(1))
            self.l1 = send(part.at[self.big(2, 2, 2)], land_big1.at[n, 1], self.step(-1))
            self.r2 = [send(part.at[self.big(1, 2, 2)], land_big2.at[n, 0, 2:4], self.step(1))]
            self.l2 = [send(part.at[self.big(-1, 0, 2)], land_big2.at[n, 1, 0:2], self.step(-1))]

        def middle(self):
            n = self.n

            def fold(way, lo, away):
                def one(i, _):
                    for q in range(2):
                        at = self.big_block(away, lo + i, q)
                        part[at] = add(part, at, (land_big1, (n, way, i, q))).astype(BF16)
                    return 0

                lax.fori_loop(0, 2, one, 0)

            self.r1.wait_recv()
            fold(0, 0, 1)
            self.r2.append(send(part.at[self.big(1, 0, 2)], land_big2.at[n, 0, 0:2], self.step(1)))
            self.l1.wait_recv()
            fold(1, 2, -1)
            self.l2.append(send(part.at[self.big(-1, 2, 2)], land_big2.at[n, 1, 2:4], self.step(-1)))

        def turn(self):
            n = self.n
            for copy in self.r2 + self.l2:
                copy.wait_recv()

            def one(i, _):
                for q in range(2):
                    at = self.big_block(0, i, q)
                    part[at] = add(part, at, (land_big2, (n, 0, i, q)), (land_big2, (n, 1, i, q))).astype(BF16)
                return 0

            lax.fori_loop(0, 4, one, 0)
            self.r3 = send(part.at[self.small(2, 0)], land_small1.at[n, 0], self.cross(1))
            self.l3 = send(part.at[self.small(2, 1)], land_small1.at[n, 1], self.cross(-1))
            self.r4 = [send(part.at[self.small(1, 1)], land_small2.at[n, 0, 1], self.cross(1))]
            self.l4 = [send(part.at[self.small(-1, 0)], land_small2.at[n, 1, 0], self.cross(-1))]

        def late(self):
            n = self.n
            self.r3.wait_recv()
            at = self.small(1, 0)
            part[at] = add(part, at, (land_small1, (n, 0))).astype(BF16)
            self.r4.append(send(part.at[at], land_small2.at[n, 0, 0], self.cross(1)))
            self.l3.wait_recv()
            at = self.small(-1, 1)
            part[at] = add(part, at, (land_small1, (n, 1))).astype(BF16)
            self.l4.append(send(part.at[at], land_small2.at[n, 1, 1], self.cross(-1)))

        def finish(self):
            n = self.n
            for copy in self.r4 + self.l4:
                copy.wait_recv()
            for q in range(2):
                value = add(part, self.small(0, q), (land_small2, (n, 0, q)), (land_small2, (n, 1, q)))
                row = (2 * self.half + q) * BS
                agg[row:row + BS, self.c * BS:(self.c + 1) * BS] = value.astype(BF16)

    reduces = [[Reduce(c, half) for half in range(2)] for c in range(2)]
    for c in range(2):
        for k in (0, 2, 1, 3):
            merge(c, k)
        for r in reduces[c]:
            r.begin()
    for stage in ("middle", "turn", "late", "finish"):
        for c in range(2):
            for r in reduces[c]:
                getattr(r, stage)()

    pre = jnp.dot(agg[...], weight_ref[...], preferred_element_type=F32)
    gate = jax.nn.sigmoid(pre)
    out_ref[...] = (pre * gate).astype(BF16)
    slope = gate * (1.0 + pre * (1.0 - gate))
    grad_pre = (cot_ref[...].astype(F32) * slope).astype(BF16)
    mixed = lax.dot_general(
        grad_pre, weight_ref[...], (((1,), (1,)), ((), ())), preferred_element_type=F32
    ).astype(BF16)
    for q in range(4):
        for c in range(2):
            grad[c][0, y, core, q] = mixed[q * BS:(q + 1) * BS, c * BS:(c + 1) * BS]

    class Gather:
        def __init__(self, c, half):
            self.c, self.half = c, half
            self.q = pl.ds(2 * half, 2)

        def at(self, first, second, q=None):
            q = self.q if q is None else 2 * self.half + q
            if self.half == 0:
                return (second & 3, near(y, first, NY), core, q)
            return (first & 3, near(y, second, NY), core, q)

        def short(self, d):
            return dev(dy=d) if self.half == 0 else dev(dx=d)

        def long(self, d):
            return dev(dx=d) if self.half == 0 else dev(dy=d)

        def hop(self, first, second, axis, d, q=None):
            there = (first - d, second) if axis == 0 else (first, second - d)
            target = self.short(d) if axis == 0 else self.long(d)
            if self.half == 0:
                there = (first, there[1]) if axis == 1 else (first, second)
            else:
                there = (there[0], second) if axis == 0 else (first, second)
            ref = grad[self.c]
            return send(ref.at[self.at(first, second, q)], ref.at[self.at(*there, q)], target)

        def begin(self):
            self.s = {d: self.hop(0, 0, 0, d) for d in (1, -1)}
            self.g = {(0, d): self.hop(0, 0, 1, d) for d in (1, -1)}

        def spread(self):
            self.s2 = {}
            for d, q in ((1, 0), (-1, 1)):
                self.s[d].wait_recv()
                self.s2[d] = self.hop(-d, 0, 0, d, q)
                for e in (1, -1):
                    self.g[-d, e] = self.hop(-d, 0, 1, e)

        def widen(self):
            for d in (1, -1):
                self.s2[d].wait_recv()
            for e in (1, -1):
                self.g[2, e] = self.hop(2, 0, 1, e)
            self.f = []
            for first in (0, -1):
                self.g[first, 1].wait_recv()
                self.f.append(self.hop(first, -1, 1, 1))

        def relay(self):
            for first in (1, 2):
                self.g[first, -1].wait_recv()
                self.f.append(self.hop(first, 1, 1, -1))
            self.share(0)

        def share(self, second):
            if self.half == 0:
                at = (second & 3, slice(None), core, self.q)
            else:
                at = (slice(None), near(y, second, NY), core, self.q)
            ref = grad[self.c]
            self.shared.append(send(ref.at[at], ref.at[at], dev(dc=1)))

        def close(self):
            for first in (1, 2):
                self.g[first, 1].wait_recv()
            self.share(-1)
            for first in (0, -1):
                self.g[first, -1].wait_recv()
            self.share(1)

        def close2(self):
            for copy in self.f:
                copy.wait_recv()
            self.share(2)

        def settle(self):
            for copy in self.shared:
                copy.wait_recv()

    gathers = [[Gather(c, half) for half in range(2)] for c in range(2)]
    for pair in gathers:
        for g in pair:
            g.shared = []

    def gather_stage(c, stage):
        for g in gathers[c]:
            getattr(g, stage)()

    gather_stage(0, "begin")

    w_terms = lax.dot_general(agg[...], grad_pre, (((0,), (0,)), ((), ())), preferred_element_type=F32)
    for p in range(NZ):
        w_mine[p] = w_terms[p * 32:(p + 1) * 32, :]
    w_z[z] = w_mine[z]
    w_copies = [
        send(w_mine.at[near(z, d, NZ)], w_z.at[z], dev(dz=d)) for d in range(1, NZ)
    ]

    gather_stage(0, "spread")
    gather_stage(1, "begin")
    gather_stage(0, "widen")

    def turn_tiles(n, _):
        for k in range(4):
            for s in range(2):
                turned[k, n, s] = held[k][n, s].T
        return 0

    lax.fori_loop(0, 8, turn_tiles, 0)

    for copy in w_copies:
        copy.wait_recv()
    total = w_z[0]
    for p in range(1, NZ):
        total = total + w_z[p]
    w_x[x] = total
    w_copies = [send(w_x.at[x], w_x.at[x], dev(dx=d)) for d in range(1, NX)]
    gather_stage(0, "relay")
    gather_stage(1, "spread")
    for copy in w_copies:
        copy.wait_recv()
    w_y[y] = (w_x[0] + w_x[1]) + (w_x[2] + w_x[3])
    w_copies = [send(w_y.at[y], w_y.at[y], dev(dy=d)) for d in range(1, NY)]
    gather_stage(0, "close")
    gather_stage(1, "widen")
    for copy in w_copies:
        copy.wait_recv()
    w_c[core] = (w_y[0] + w_y[1]) + (w_y[2] + w_y[3])
    w_copy = send(w_c.at[core], w_c.at[core], dev(dc=1))
    gather_stage(0, "close2")
    gather_stage(1, "relay")
    w_copy.wait_recv()
    w_all[z] = (w_c[0] + w_c[1]) * (1.0 / math.sqrt(NZ * NX * NY * NC * 4 * BS))
    w_copies = [send(w_all.at[z], w_all.at[z], dev(dz=d)) for d in range(1, NZ)]
    gather_stage(0, "settle")

    def backward(c, slot, store):
        for k in range(4):
            m = (slot - lax.div(x + k, jnp.int32(NX))) & 7
            for s in range(2):
                n = k * 2 + s
                at = m * 8 + n
                row, col = meta_s[k, 4, at] & 31, meta_s[k, 5, at]
                tile = turned[k, m, s]
                for q in range(4):
                    lhs[q * BS:(q + 1) * BS, n * BS:(n + 1) * BS] = tile * jnp.where(col == q, 1, 0).astype(BF16)
                rhs[n * BS:(n + 1) * BS, :] = grad[c][k, row >> 3, (row >> 2) & 1, row & 3]
        value = jnp.dot(lhs[...], rhs[...], preferred_element_type=F32)
        for q in range(4):
            store[q] = value[q * BS:(q + 1) * BS, :]

    class Back:
        def __init__(self, c):
            self.c = c

        def begin(self):
            c = self.c
            backward(c, jnp.int32(4), terms.at[0])
            for way in range(2):
                for q in range(2):
                    z_out[c, way, 0, 2 * way + q] = terms[0, 2 * way + q].astype(BF16)
            self.copies = [
                send(z_out.at[c, way, 0, pl.ds(2 * way, 2)], z_in.at[c, way, 0, pl.ds(2 * way, 2)], dev(dz=1 - 2 * way))
                for way in range(2)
            ]

        def step(self, t):
            c = self.c
            away = 4 - t

            def one(way, _):
                backward(c, jnp.where(way == 0, 8 - away, away), terms.at[way])
                return 0

            lax.fori_loop(0, 2, one, 0)
            copies = []
            for way in range(2):
                self.copies[way].wait_recv()
                for q in range(4):
                    value = terms[way, q]
                    if t > 1 or q // 2 == way:
                        value = value + z_in[c, way, t - 1, q].astype(F32)
                    z_out[c, way, t, q] = value.astype(BF16)
                copies.append(send(z_out.at[c, way, t], z_in.at[c, way, t], dev(dz=1 - 2 * way)))
            self.copies = copies

        def finish(self):
            c = self.c
            backward(c, jnp.int32(0), terms.at[0])
            for copy in self.copies:
                copy.wait_recv()
            for q in range(4):
                value = terms[0, q] + z_in[c, 0, 3, q].astype(F32) + z_in[c, 1, 3, q].astype(F32)
                gfeat_ref[q * BS:(q + 1) * BS, c * BS:(c + 1) * BS] = value.astype(BF16)

    backs = [Back(0), Back(1)]
    backs[0].begin()
    gather_stage(1, "close")
    backs[0].step(1)
    gather_stage(1, "close2")
    backs[0].step(2)
    gather_stage(1, "settle")
    backs[1].begin()
    backs[0].step(3)
    backs[1].step(1)
    for copy in w_copies:
        copy.wait_recv()
    for p in range(NZ):
        gweight_ref[p * 32:(p + 1) * 32, :] = w_all[p]
    backs[0].finish()
    backs[1].step(2)
    backs[1].step(3)
    backs[1].finish()
    for copy in started:
        copy.wait_send()


def body(features, weight, tiles, tile_place, tile_count, cotangent):
    rows, width = features.shape
    tiles = tiles.reshape(8, 4, 2, BS, BS)
    live = jnp.arange(2)[None, :] < tile_count[0][:, None]
    code = (tile_place[0] + jnp.where(live, 128, 0)).reshape(64)
    code = jnp.broadcast_to(jnp.concatenate([code, jnp.zeros((64,), jnp.int32)])[:, None], (BS, BS))
    vmem = pl.BlockSpec(memory_space=pltpu.VMEM)
    bf = lambda *lead: pltpu.VMEM(lead + (BS, BS), BF16)
    f32 = lambda *shape: pltpu.VMEM(shape, F32)
    scratch = [
        pltpu.VMEM((8, 4, BS, 2 * BS), BF16),
        bf(8, 2), bf(8, 2), bf(8, 2), bf(8, 2),
        bf(2, 4, 2),
        pltpu.VMEM((4, 8, BS), jnp.int32), pltpu.SMEM((4, 8, BS), jnp.int32),
        f32(17, BS, 2 * BS),
        bf(2, 4, 4, 2, 4), bf(2, 4, 4, 4),
        bf(4, 2, 2, 2), bf(4, 2, 4, 2), bf(4, 2), bf(4, 2, 2),
        pltpu.VMEM((4 * BS, 2 * BS), BF16),
        bf(4, 4, 2, 4), bf(4, 4, 2, 4),
        bf(4, 8, 2),
        pltpu.VMEM((4 * BS, 8 * BS), BF16), pltpu.VMEM((8 * BS, BS), BF16),
        f32(2, 4, BS, BS),
        bf(2, 2, 4, 4), bf(2, 2, 4, 4),
        f32(8, 32, 2 * BS), f32(8, 32, 2 * BS), f32(4, 32, 2 * BS), f32(4, 32, 2 * BS),
        f32(2, 32, 2 * BS), f32(8, 32, 2 * BS),
        pltpu.SemaphoreType.DMA((SEM_TOTAL,)), pltpu.SemaphoreType.DMA((SEM_TOTAL,)),
        pltpu.SemaphoreType.DMA, pltpu.SemaphoreType.DMA,
    ]
    return pl.pallas_call(
        kernel,
        out_shape=(
            jax.ShapeDtypeStruct((rows, width), BF16),
            jax.ShapeDtypeStruct((rows, width), BF16),
            jax.ShapeDtypeStruct((width, width), F32),
        ),
        in_specs=[vmem] * 5,
        out_specs=(vmem,) * 3,
        scratch_shapes=scratch,
        compiler_params=pltpu.CompilerParams(
            collective_id=0, has_side_effects=True, vmem_limit_bytes=56 * 1024 * 1024
        ),
    )(features, weight, tiles, code, cotangent)


def solution(mesh):
    return jax.shard_map(
        body,
        mesh=mesh,
        in_specs=(
            P(("blk", "rep"), None),
            P(),
            P(("blk", "rep"), None, None, None, None),
            P(("blk", "rep"), None, None),
            P(("blk", "rep"), None),
            P(("blk", "rep"), None),
        ),
        out_specs=(P(("blk", "rep"), None), P(("blk", "rep"), None), P()),
        check_vma=False,
    )
```

```python
import functools
import math

import jax
import jax.numpy as jnp
from jax import lax
from jax.experimental import pallas as pl
from jax.experimental.pallas import tpu as pltpu
from jax.sharding import PartitionSpec as P

NZ, NX, NY, NC = 8, 4, 4, 2
BS = 128
F32, BF16 = jnp.float32, jnp.bfloat16
SEM_TOTAL = 320
SPOT = (0, 2, 1, 3)


def rem(a, n):
    return lax.rem(a, jnp.int32(n))


def kernel(
    feat_ref, weight_ref, tiles_ref, place_ref, count_ref, cot_ref,
    out_ref, gfeat_ref, gweight_ref,
    feats, held0, held1, held2, held3, passing, meta, meta_s, sums, part, sib,
    land_big1, land_big2, land_small,
    agg, grad0, grad1, turned, lhs, rhs, terms, z_out, z_in,
    w_mine, w_z, w_x, w_y, w_c, w_all,
    send_sem, recv_sem, local_sem, meta_sem,
):
    blk, rep = lax.axis_index("blk"), lax.axis_index("rep")
    z, x = lax.div(blk, jnp.int32(NX)), rem(blk, NX)
    y, core = lax.div(rep, jnp.int32(NC)), rem(rep, NC)

    held, grad = (held0, held1, held2, held3), (grad0, grad1)

    def dev(dz=0, dx=0, dy=0, dc=0):
        return {
            "blk": rem(z + dz + NZ, NZ) * NX + rem(x + dx + NX, NX),
            "rep": rem(y + dy + NY, NY) * NC + rem(core + dc, NC),
        }

    peers = [dev(dc=1)]
    peers += [dev(dx=d) for d in range(1, NX)]
    peers += [dev(dy=d) for d in range(1, NY)]
    peers += [dev(dz=d) for d in range(1, NZ)]
    started = []

    def send(src, dst, target):
        n = len(started)
        copy = pltpu.make_async_remote_copy(
            src_ref=src, dst_ref=dst, send_sem=send_sem.at[n], recv_sem=recv_sem.at[n],
            device_id=target, device_id_type=pl.DeviceIdType.MESH,
        )
        copy.start()
        started.append(copy)
        return copy

    own_tiles = pltpu.make_async_copy(tiles_ref.at[:, 0], held[0], local_sem)
    own_tiles.start()

    barrier = pltpu.get_barrier_semaphore()
    for peer in peers:
        pl.semaphore_signal(barrier, inc=1, device_id=peer, device_id_type=pl.DeviceIdType.MESH)

    for q in range(4):
        feats[0, q] = feat_ref[q * BS:(q + 1) * BS, :]

    pl.semaphore_wait(barrier, len(peers))

    around = {}

    def pass_on(step):
        for half in range(2):
            rows = pl.ds(2 * half, 2)
            for way in (1, -1):
                if step == 3 and half != (way < 0):
                    continue
                if step:
                    around[step - 1, half, way].wait_recv()
                here, there = (way * step) & 7, (way * (step + 1)) & 7
                around[step, half, way] = send(feats.at[here, rows], feats.at[there, rows], dev(dz=way))

    pass_on(0)
    tile_a = send(tiles_ref.at[0:4, 2], passing.at[0], dev(dx=1))
    tile_b = send(tiles_ref.at[4:8, 2], passing.at[1], dev(dx=-1))

    ids = lax.broadcasted_iota(jnp.int32, (BS, BS), 0)
    lanes = lax.broadcasted_iota(jnp.int32, (BS, BS), 1)
    unused = jnp.zeros((1, 64), jnp.int32)
    places = jnp.concatenate([place_ref[0:1, :], place_ref[1:2, :], unused], axis=1)
    counts = jnp.concatenate([count_ref[...], count_ref[...], unused], axis=1)
    places, counts = jnp.broadcast_to(places, (BS, BS)), jnp.broadcast_to(counts, (BS, BS))
    flipped = places + jnp.where(counts > (lanes >> 5), 128, 0)
    code = flipped.T

    def parts_of(value, at):
        inside = at < 64
        live = jnp.logical_and(value >= 128, inside)
        group = jnp.where(inside, at & 3, -1)
        row = jnp.where(live, (value & 127) >> 2, 32)
        return live, group, row, value & 3

    live_e, group_e, row_e, col_e = parts_of(code, ids)
    live_f, group_f, row_f, col_f = parts_of(flipped, lanes)
    key_e, key_f = row_e * 64 + ids, row_f * 64 + lanes
    before = jnp.logical_and(jnp.logical_and(group_e == group_f, lanes < 64), key_f < key_e)

    def count(flags, axis):
        return jnp.sum(jnp.where(flags, 1, 0), axis=axis, keepdims=True)

    rank = count(before, 1)
    same = count(jnp.logical_and(before, row_e == row_f), 1)
    chosen = jnp.logical_and(
        jnp.logical_and(group_e == (lanes >> 4), ids < 64), rank == (lanes & 15)
    )
    entry = ((ids >> 2) & 7) * 2 + (ids >> 5)
    meta[0, 0:1, :] = jnp.sum(jnp.where(chosen, entry, 0), axis=0, keepdims=True)
    meta[0, 1:2, :] = jnp.sum(jnp.where(chosen, col_e, 0), axis=0, keepdims=True)
    meta[0, 2:3, :] = count(jnp.logical_and(chosen, same == 0), 0)
    mine = jnp.logical_and(live_e, group_e == (lanes >> 5))
    here = count(jnp.logical_and(mine, row_e == (lanes & 31)), 0)
    upto = count(jnp.logical_and(mine, row_e <= (lanes & 31)), 0)
    meta[0, 3:4, :] = jnp.where(here > 0, upto - 1, 16)
    meta[0, 4:5, :] = jnp.where(live_f, row_f, 0)[0:1, :]
    meta[0, 5:6, :] = jnp.where(live_f, col_f, 4)[0:1, :]
    meta[0, 6:8, :] = jnp.zeros((2, BS), jnp.int32)
    meta_copies = [send(meta.at[0], meta.at[k], dev(dx=-k)) for k in (1, 2, 3)]
    sums[16] = jnp.zeros((BS, 2 * BS), F32)

    pass_on(1)
    tile_a.wait_recv()
    tile_fa = send(passing.at[0], held[2].at[0:4], dev(dx=1))
    tile_b.wait_recv()
    tile_fb = send(passing.at[1], held[2].at[4:8], dev(dx=-1))
    tile_1 = send(tiles_ref.at[:, 1], held[1], dev(dx=-1))
    tile_3 = send(tiles_ref.at[:, 3], held[3], dev(dx=1))
    pass_on(2)
    for copy in meta_copies:
        copy.wait_recv()
    to_s = pltpu.make_async_copy(meta, meta_s, meta_sem)
    to_s.start()
    own_tiles.wait()

    def turn(k):
        def one(n, _):
            for s in range(2):
                turned[k, n, s] = held[k][n, s].T
            return 0

        lax.fori_loop(0, 8, one, 0)

    turn(0)
    pass_on(3)
    to_s.wait()
    for key in ((2, 0, -1), (2, 1, 1), (3, 0, 1), (3, 1, -1)):
        around[key].wait_recv()

    sib_copies = {}

    def forward(k):
        carry = lax.div(x + k, jnp.int32(NX))

        def four(g, total):
            for u in range(4):
                at = k * 16 + g * 4 + u
                e, col, fresh = meta_s[k, 0, at] & 15, meta_s[k, 1, at] & 3, meta_s[k, 2, at]
                product = jnp.dot(
                    held[k][e >> 1, e & 1], feats[((e >> 1) + carry) & 7, col], preferred_element_type=F32
                )
                total = product + total * (1 - fresh).astype(F32)
                sums[g * 4 + u] = total
            return total

        lax.fori_loop(0, 4, four, jnp.zeros((BS, 2 * BS), F32))

        def place(i, _):
            for cc in range(2):
                for q in range(4):
                    row = (i * 2 + cc) * 4 + q
                    value = sums[jnp.clip(meta_s[k, 3, k * 32 + row], 0, 16)].astype(BF16)
                    part[0, SPOT[k], i, cc, q] = value[:, :BS]
                    part[1, SPOT[k], i, cc, q] = value[:, BS:]
            return 0

        lax.fori_loop(0, 4, place, 0)
        for c in range(2):
            sib_copies[c, k] = send(part.at[c, SPOT[k], :, 1 - core], sib.at[c, SPOT[k]], dev(dc=1))

    def add(ref, index, *others):
        value = ref[index].astype(F32)
        for other, at in others:
            value = value + other[at].astype(F32)
        return value

    def merge(c, k):
        sib_copies[c, k].wait_recv()
        at = SPOT[k]

        def one(i, _):
            part[c, at, i, core] = part[c, at, i, core] + sib[c, at, i]
            return 0

        lax.fori_loop(0, NY, one, 0)

    def near(value, step, size):
        return rem(value + step + size, size)

    class Reduce:
        def __init__(self, c, half):
            self.c, self.half = c, half
            self.n = c * 2 + half

        def step(self, d):
            return dev(dx=d) if self.half == 0 else dev(dy=d)

        def cross(self, d):
            return dev(dy=d) if self.half == 0 else dev(dx=d)

        def big(self, away, lo, size):
            q = pl.ds(2 * self.half, 2)
            if self.half == 0:
                return (self.c, SPOT[away & 3], pl.ds(lo, size), core, q)
            return (self.c, pl.ds(lo, size), near(y, away, NY), core, q)

        def big_block(self, away, at, q):
            if self.half == 0:
                return (self.c, SPOT[away & 3], at, core, q)
            return (self.c, at, near(y, away, NY), core, 2 + q)

        def small(self, away, q, whole=False):
            if self.half == 0:
                return (self.c, 0, near(y, away, NY), core, q)
            return (self.c, SPOT[away & 3], y, core, pl.ds(2, 2) if whole else 2 + q)

        def far_r(self):
            self.r1 = send(part.at[self.big(2, 0, 2)], land_big1.at[self.n, 0], self.step(1))

        def far_l(self):
            self.l1 = send(part.at[self.big(2, 2, 2)], land_big1.at[self.n, 1], self.step(-1))

        def next_r(self):
            self.r2 = [send(part.at[self.big(1, 2, 2)], land_big2.at[self.n, 0, 2:4], self.step(1))]

        def next_l(self):
            self.l2 = [send(part.at[self.big(-1, 0, 2)], land_big2.at[self.n, 1, 0:2], self.step(-1))]

        def middle(self):
            n = self.n

            def fold(way, lo, away):
                def one(i, _):
                    for q in range(2):
                        at = self.big_block(away, lo + i, q)
                        part[at] = part[at] + land_big1[n, way, i, q]
                    return 0

                lax.fori_loop(0, 2, one, 0)

            self.r1.wait_recv()
            fold(0, 0, 1)
            self.r2.append(send(part.at[self.big(1, 0, 2)], land_big2.at[n, 0, 0:2], self.step(1)))
            self.l1.wait_recv()
            fold(1, 2, -1)
            self.l2.append(send(part.at[self.big(-1, 2, 2)], land_big2.at[n, 1, 2:4], self.step(-1)))

        def turn(self):
            n = self.n
            for copy in self.r2 + self.l2:
                copy.wait_recv()

            def one(i, _):
                for q in range(2):
                    at = self.big_block(0, i, q)
                    part[at] = add(part, at, (land_big2, (n, 0, i, q)), (land_big2, (n, 1, i, q))).astype(BF16)
                return 0

            lax.fori_loop(0, 4, one, 0)
            self.last = [
                send(part.at[self.small(d, pl.ds(0, 2), whole=True)], land_small.at[n, d - 1], self.cross(d))
                for d in (2, 1, 3)
            ]

        def finish(self):
            n = self.n
            for copy in self.last:
                copy.wait_recv()
            for q in range(2):
                value = add(part, self.small(0, q), *[(land_small, (n, d, q)) for d in range(3)])
                row = (2 * self.half + q) * BS
                agg[row:row + BS, self.c * BS:(self.c + 1) * BS] = value.astype(BF16)

    reduces = [[Reduce(c, half) for half in range(2)] for c in range(2)]
    forward(0)
    tile_fa.wait_recv()
    tile_fb.wait_recv()
    forward(2)
    for c in range(2):
        merge(c, 0)
        merge(c, 2)
        reduces[c][1].far_r()
        reduces[c][0].far_r()
        reduces[c][0].far_l()
        reduces[c][1].next_l()
    tile_1.wait_recv()
    forward(1)
    tile_3.wait_recv()
    forward(3)
    for c in range(2):
        merge(c, 1)
        reduces[c][0].next_r()
        merge(c, 3)
        reduces[c][1].far_l()
        reduces[c][1].next_r()
        reduces[c][0].next_l()
    turn(2)
    turn(1)
    turn(3)
    for stage in ("middle", "turn", "finish"):
        for c in range(2):
            for r in reduces[c]:
                getattr(r, stage)()

    pre = jnp.dot(agg[...], weight_ref[...], preferred_element_type=F32)
    gate = jax.nn.sigmoid(pre)
    out_ref[...] = (pre * gate).astype(BF16)
    slope = gate * (1.0 + pre * (1.0 - gate))
    grad_pre = (cot_ref[...].astype(F32) * slope).astype(BF16)
    mixed = lax.dot_general(
        grad_pre, weight_ref[...], (((1,), (1,)), ((), ())), preferred_element_type=F32
    ).astype(BF16)
    for q in range(4):
        for c in range(2):
            grad[c][0, y, core, q] = mixed[q * BS:(q + 1) * BS, c * BS:(c + 1) * BS]

    class Gather:
        def __init__(self, c, half):
            self.c, self.half = c, half
            self.q = pl.ds(2 * half, 2)

        def at(self, first, second, q=None):
            q = self.q if q is None else 2 * self.half + q
            if self.half == 0:
                return (second & 3, near(y, first, NY), core, q)
            return (first & 3, near(y, second, NY), core, q)

        def short(self, d):
            return dev(dy=d) if self.half == 0 else dev(dx=d)

        def long(self, d):
            return dev(dx=d) if self.half == 0 else dev(dy=d)

        def hop(self, first, second, axis, d, q=None):
            there = (first - d, second) if axis == 0 else (first, second - d)
            target = self.short(d) if axis == 0 else self.long(d)
            if self.half == 0:
                there = (first, there[1]) if axis == 1 else (first, second)
            else:
                there = (there[0], second) if axis == 0 else (first, second)
            ref = grad[self.c]
            return send(ref.at[self.at(first, second, q)], ref.at[self.at(*there, q)], target)

        def begin(self):
            self.s = {d: self.hop(0, 0, 0, d) for d in (1, -1, 2)}
            self.g = {(0, d): self.hop(0, 0, 1, d) for d in (1, -1)}

        def spread(self):
            for d in (1, -1, 2):
                self.s[d].wait_recv()
                for e in (1, -1):
                    self.g[2 if d == 2 else -d, e] = self.hop(-d, 0, 1, e)

        def relay(self):
            self.f = []
            for first in (0, -1):
                self.g[first, 1].wait_recv()
                self.f.append(self.hop(first, -1, 1, 1))
            for first in (1, 2):
                self.g[first, -1].wait_recv()
                self.f.append(self.hop(first, 1, 1, -1))
            self.share(0)

        def share(self, second):
            if self.half == 0:
                at = (second & 3, slice(None), core, self.q)
            else:
                at = (slice(None), near(y, second, NY), core, self.q)
            ref = grad[self.c]
            self.shared.append(send(ref.at[at], ref.at[at], dev(dc=1)))

        def close(self):
            for first in (1, 2):
                self.g[first, 1].wait_recv()
            self.share(-1)
            for first in (0, -1):
                self.g[first, -1].wait_recv()
            self.share(1)

        def close2(self):
            for copy in self.f:
                copy.wait_recv()
            self.share(2)

        def settle(self):
            for copy in self.shared:
                copy.wait_recv()

    gathers = [[Gather(c, half) for half in range(2)] for c in range(2)]
    for pair in gathers:
        for g in pair:
            g.shared = []

    def gather_stage(c, stage):
        for g in gathers[c]:
            getattr(g, stage)()

    gather_stage(0, "begin")

    w_terms = lax.dot_general(agg[...], grad_pre, (((0,), (0,)), ((), ())), preferred_element_type=F32)
    for p in range(NZ):
        w_mine[p] = w_terms[p * 32:(p + 1) * 32, :].astype(BF16)
    w_z[z] = w_mine[z]
    w_copies = [
        send(w_mine.at[near(z, d, NZ)], w_z.at[z], dev(dz=d)) for d in range(1, NZ)
    ]

    gather_stage(0, "spread")
    gather_stage(1, "begin")
    gather_stage(0, "relay")
    gather_stage(0, "close")
    gather_stage(1, "spread")
    for copy in w_copies:
        copy.wait_recv()
    total = w_z[0].astype(F32)
    for p in range(1, NZ):
        total = total + w_z[p].astype(F32)
    w_x[x] = total
    w_copies = [send(w_x.at[x], w_x.at[x], dev(dx=d)) for d in range(1, NX)]
    gather_stage(0, "close2")
    gather_stage(1, "relay")
    gather_stage(0, "settle")
    for copy in w_copies:
        copy.wait_recv()
    w_y[y] = (w_x[0] + w_x[1]) + (w_x[2] + w_x[3])
    w_copies = [send(w_y.at[y], w_y.at[y], dev(dy=d)) for d in range(1, NY)]

    def backward(c, slot, store):
        for k in range(4):
            m = (slot - lax.div(x + k, jnp.int32(NX))) & 7
            for s in range(2):
                n = k * 2 + s
                at = s * 32 + m * 4 + k
                row, col = meta_s[k, 4, at] & 31, meta_s[k, 5, at]
                tile = turned[k, m, s]
                for q in range(4):
                    lhs[q * BS:(q + 1) * BS, n * BS:(n + 1) * BS] = tile * jnp.where(col == q, 1, 0).astype(BF16)
                rhs[n * BS:(n + 1) * BS, :] = grad[c][k, row >> 3, (row >> 2) & 1, row & 3]
        value = jnp.dot(lhs[...], rhs[...], preferred_element_type=F32)
        for q in range(4):
            store[q] = value[q * BS:(q + 1) * BS, :]

    class Back:
        def __init__(self, c):
            self.c = c

        def put(self, way, t, q, value):
            c = self.c
            z_out[c, way, t, q] = value.astype(BF16)
            self.copies[way, t, q] = send(z_out.at[c, way, t, q], z_in.at[c, way, t, q], dev(dz=1 - 2 * way))

        def begin(self):
            self.copies = {}
            backward(self.c, jnp.int32(4), terms.at[0])
            for q in range(2):
                for way in range(2):
                    self.put(way, 0, 2 * way + q, terms[0, 2 * way + q])

        def step(self, t):
            c = self.c
            away = 4 - t

            def one(way, _):
                backward(c, jnp.where(way == 0, 8 - away, away), terms.at[way])
                return 0

            lax.fori_loop(0, 2, one, 0)
            for q in range(4):
                for way in range(2):
                    at = (q + 2 * (1 - way)) & 3
                    value = terms[way, at]
                    if (way, t - 1, at) in self.copies:
                        self.copies[way, t - 1, at].wait_recv()
                        value = value + z_in[c, way, t - 1, at].astype(F32)
                    self.put(way, t, at, value)

        def finish(self):
            c = self.c
            backward(c, jnp.int32(0), terms.at[0])
            for n in range(4):
                q = (n + 2) & 3
                value = terms[0, q]
                for way in range(2):
                    self.copies[way, 3, q].wait_recv()
                    value = value + z_in[c, way, 3, q].astype(F32)
                gfeat_ref[q * BS:(q + 1) * BS, c * BS:(c + 1) * BS] = value.astype(BF16)

    backs = [Back(0), Back(1)]
    backs[0].begin()
    gather_stage(1, "close")
    for copy in w_copies:
        copy.wait_recv()
    w_c[core] = (w_y[0] + w_y[1]) + (w_y[2] + w_y[3])
    w_copy = send(w_c.at[core], w_c.at[core], dev(dc=1))
    backs[0].step(1)
    gather_stage(1, "close2")
    w_copy.wait_recv()
    w_all[z] = ((w_c[0] + w_c[1]) * (1.0 / math.sqrt(NZ * NX * NY * NC * 4 * BS))).astype(BF16)
    w_copies = [send(w_all.at[z], w_all.at[z], dev(dz=d)) for d in range(1, NZ)]
    gather_stage(1, "settle")
    backs[1].begin()
    backs[0].step(2)
    backs[1].step(1)
    backs[0].step(3)
    backs[1].step(2)
    for copy in w_copies:
        copy.wait_recv()
    for p in range(NZ):
        gweight_ref[p * 32:(p + 1) * 32, :] = w_all[p].astype(F32)
    backs[0].finish()
    backs[1].step(3)
    backs[1].finish()
    for copy in started:
        copy.wait_send()


def hand_over(*refs):
    for source, result in zip(refs[:3], refs[3:]):
        result[...] = source[...]


def body(features, weight, tiles, tile_place, tile_count, cotangent):
    rows, width = features.shape
    tiles = tiles.reshape(8, 4, 2, BS, BS)
    vmem = pl.BlockSpec(memory_space=pltpu.VMEM)
    bf = lambda *lead: pltpu.VMEM(lead + (BS, BS), BF16)
    f32 = lambda *shape: pltpu.VMEM(shape, F32)
    scratch = [
        pltpu.VMEM((8, 4, BS, 2 * BS), BF16),
        bf(8, 2), bf(8, 2), bf(8, 2), bf(8, 2),
        bf(2, 4, 2),
        pltpu.VMEM((4, 8, BS), jnp.int32), pltpu.SMEM((4, 8, BS), jnp.int32),
        f32(17, BS, 2 * BS),
        bf(2, 4, 4, 2, 4), bf(2, 4, 4, 4),
        bf(4, 2, 2, 2), bf(4, 2, 4, 2), bf(4, 3, 2),
        pltpu.VMEM((4 * BS, 2 * BS), BF16),
        bf(4, 4, 2, 4), bf(4, 4, 2, 4),
        bf(4, 8, 2),
        pltpu.VMEM((4 * BS, 8 * BS), BF16), pltpu.VMEM((8 * BS, BS), BF16),
        f32(2, 4, BS, BS),
        bf(2, 2, 4, 4), bf(2, 2, 4, 4),
        pltpu.VMEM((8, 32, 2 * BS), BF16), pltpu.VMEM((8, 32, 2 * BS), BF16),
        f32(4, 32, 2 * BS), f32(4, 32, 2 * BS), f32(2, 32, 2 * BS),
        pltpu.VMEM((8, 32, 2 * BS), BF16),
        pltpu.SemaphoreType.DMA((SEM_TOTAL,)), pltpu.SemaphoreType.DMA((SEM_TOTAL,)),
        pltpu.SemaphoreType.DMA, pltpu.SemaphoreType.DMA,
    ]
    shapes = (
        jax.ShapeDtypeStruct((rows, width), BF16),
        jax.ShapeDtypeStruct((rows, width), BF16),
        jax.ShapeDtypeStruct((width, width), F32),
    )
    results = pl.pallas_call(
        kernel,
        out_shape=shapes,
        in_specs=[vmem] * 6,
        out_specs=(vmem,) * 3,
        scratch_shapes=scratch,
        compiler_params=pltpu.CompilerParams(
            collective_id=0, has_side_effects=True, vmem_limit_bytes=56 * 1024 * 1024
        ),
    )(features, weight, tiles, tile_place[0].T, tile_count, cotangent)
    return pl.pallas_call(
        hand_over, out_shape=shapes, in_specs=[vmem] * 3, out_specs=(vmem,) * 3
    )(*results)


def solution(mesh):
    return jax.shard_map(
        body,
        mesh=mesh,
        in_specs=(
            P(("blk", "rep"), None),
            P(),
            P(("blk", "rep"), None, None, None, None),
            P(("blk", "rep"), None, None),
            P(("blk", "rep"), None),
            P(("blk", "rep"), None),
        ),
        out_specs=(P(("blk", "rep"), None), P(("blk", "rep"), None), P()),
        check_vma=False,
    )
```

```python
import functools
import math

import jax
import jax.numpy as jnp
from jax import lax
from jax.experimental import pallas as pl
from jax.experimental.pallas import tpu as pltpu
from jax.sharding import PartitionSpec as P

NZ, NX, NY, NC = 8, 4, 4, 2
BS = 128
F32, BF16 = jnp.float32, jnp.bfloat16
SEM_TOTAL = 320
SPOT = (0, 2, 1, 3)


def rem(a, n):
    return lax.rem(a, jnp.int32(n))


def kernel(
    feat_ref, weight_ref, tiles_ref, place_ref, count_ref, cot_ref,
    out_ref, gfeat_ref, gweight_ref,
    feats, held0, held1, held2, held3, passing, meta, meta_s, sums, part, sib,
    land_big1, land_big2, land_small,
    agg, grad0, grad1, turned, lhs, rhs, terms, z_out, z_in,
    w_mine, w_sib, w_half, w_z, w_x, w_y, w_all,
    send_sem, recv_sem, local_sem, meta_sem,
):
    blk, rep = lax.axis_index("blk"), lax.axis_index("rep")
    z, x = lax.div(blk, jnp.int32(NX)), rem(blk, NX)
    y, core = lax.div(rep, jnp.int32(NC)), rem(rep, NC)

    held, grad = (held0, held1, held2, held3), (grad0, grad1)

    def dev(dz=0, dx=0, dy=0, dc=0):
        return {
            "blk": rem(z + dz + NZ, NZ) * NX + rem(x + dx + NX, NX),
            "rep": rem(y + dy + NY, NY) * NC + rem(core + dc, NC),
        }

    peers = [dev(dc=1)]
    peers += [dev(dx=d) for d in range(1, NX)]
    peers += [dev(dy=d) for d in range(1, NY)]
    peers += [dev(dz=d) for d in range(1, NZ)]
    started = []

    def send(src, dst, target):
        n = len(started)
        copy = pltpu.make_async_remote_copy(
            src_ref=src, dst_ref=dst, send_sem=send_sem.at[n], recv_sem=recv_sem.at[n],
            device_id=target, device_id_type=pl.DeviceIdType.MESH,
        )
        copy.start()
        started.append(copy)
        return copy

    own_tiles = pltpu.make_async_copy(tiles_ref.at[:, 0], held[0], local_sem)
    own_tiles.start()

    barrier = pltpu.get_barrier_semaphore()
    for peer in peers:
        pl.semaphore_signal(barrier, inc=1, device_id=peer, device_id_type=pl.DeviceIdType.MESH)

    for q in range(4):
        feats[0, q] = feat_ref[q * BS:(q + 1) * BS, :]

    pl.semaphore_wait(barrier, len(peers))

    around = {}

    def pass_on(step):
        for half in range(2):
            rows = pl.ds(2 * half, 2)
            for way in (1, -1):
                if step == 3 and half != (way < 0):
                    continue
                if step:
                    around[step - 1, half, way].wait_recv()
                here, there = (way * step) & 7, (way * (step + 1)) & 7
                around[step, half, way] = send(feats.at[here, rows], feats.at[there, rows], dev(dz=way))

    pass_on(0)
    tile_a = send(tiles_ref.at[0:4, 2], passing.at[0], dev(dx=1))
    tile_b = send(tiles_ref.at[4:8, 2], passing.at[1], dev(dx=-1))

    ids = lax.broadcasted_iota(jnp.int32, (BS, BS), 0)
    lanes = lax.broadcasted_iota(jnp.int32, (BS, BS), 1)
    unused = jnp.zeros((1, 64), jnp.int32)
    places = jnp.concatenate([place_ref[0:1, :], place_ref[1:2, :], unused], axis=1)
    counts = jnp.concatenate([count_ref[...], count_ref[...], unused], axis=1)
    places, counts = jnp.broadcast_to(places, (BS, BS)), jnp.broadcast_to(counts, (BS, BS))
    flipped = places + jnp.where(counts > (lanes >> 5), 128, 0)
    code = flipped.T

    def parts_of(value, at):
        inside = at < 64
        live = jnp.logical_and(value >= 128, inside)
        group = jnp.where(inside, at & 3, -1)
        row = jnp.where(live, (value & 127) >> 2, 32)
        return live, group, row, value & 3

    live_e, group_e, row_e, col_e = parts_of(code, ids)
    live_f, group_f, row_f, col_f = parts_of(flipped, lanes)
    key_e, key_f = row_e * 64 + ids, row_f * 64 + lanes
    before = jnp.logical_and(jnp.logical_and(group_e == group_f, lanes < 64), key_f < key_e)

    def count(flags, axis):
        return jnp.sum(jnp.where(flags, 1, 0), axis=axis, keepdims=True)

    rank = count(before, 1)
    same = count(jnp.logical_and(before, row_e == row_f), 1)
    chosen = jnp.logical_and(
        jnp.logical_and(group_e == (lanes >> 4), ids < 64), rank == (lanes & 15)
    )
    entry = ((ids >> 2) & 7) * 2 + (ids >> 5)
    meta[0, 0:1, :] = jnp.sum(jnp.where(chosen, entry, 0), axis=0, keepdims=True)
    meta[0, 1:2, :] = jnp.sum(jnp.where(chosen, col_e, 0), axis=0, keepdims=True)
    meta[0, 2:3, :] = count(jnp.logical_and(chosen, same == 0), 0)
    mine = jnp.logical_and(live_e, group_e == (lanes >> 5))
    here = count(jnp.logical_and(mine, row_e == (lanes & 31)), 0)
    upto = count(jnp.logical_and(mine, row_e <= (lanes & 31)), 0)
    meta[0, 3:4, :] = jnp.where(here > 0, upto - 1, 16)
    meta[0, 4:5, :] = jnp.where(live_f, row_f, 0)[0:1, :]
    meta[0, 5:6, :] = jnp.where(live_f, col_f, 4)[0:1, :]
    meta[0, 6:8, :] = jnp.zeros((2, BS), jnp.int32)
    meta_copies = [send(meta.at[0], meta.at[k], dev(dx=-k)) for k in (1, 2, 3)]
    sums[16] = jnp.zeros((BS, 2 * BS), BF16)

    pass_on(1)
    tile_a.wait_recv()
    tile_fa = send(passing.at[0], held[2].at[0:4], dev(dx=1))
    tile_b.wait_recv()
    tile_fb = send(passing.at[1], held[2].at[4:8], dev(dx=-1))
    tile_1 = send(tiles_ref.at[:, 1], held[1], dev(dx=-1))
    tile_3 = send(tiles_ref.at[:, 3], held[3], dev(dx=1))
    pass_on(2)
    for copy in meta_copies:
        copy.wait_recv()
    to_s = pltpu.make_async_copy(meta, meta_s, meta_sem)
    to_s.start()
    own_tiles.wait()

    def turn(k):
        def one(n, _):
            for s in range(2):
                turned[k, n, s] = held[k][n, s].T
            return 0

        lax.fori_loop(0, 8, one, 0)

    turn(0)
    pass_on(3)
    to_s.wait()
    for key in ((2, 0, -1), (2, 1, 1), (3, 0, 1), (3, 1, -1)):
        around[key].wait_recv()

    sib_copies = {}

    def forward(k):
        carry = lax.div(x + k, jnp.int32(NX))

        def four(g, total):
            for u in range(4):
                at = k * 16 + g * 4 + u
                e, col, fresh = meta_s[k, 0, at] & 15, meta_s[k, 1, at] & 3, meta_s[k, 2, at]
                product = jnp.dot(
                    held[k][e >> 1, e & 1], feats[((e >> 1) + carry) & 7, col], preferred_element_type=F32
                )
                total = product + total * (1 - fresh).astype(F32)
                sums[g * 4 + u] = total.astype(BF16)
            return total

        total = jnp.zeros((BS, 2 * BS), F32)
        for g in range(4):
            total = four(g, total)

        def place(i, _):
            for cc in range(2):
                for q in range(4):
                    row = (i * 2 + cc) * 4 + q
                    value = sums[jnp.clip(meta_s[k, 3, k * 32 + row], 0, 16)]
                    part[0, SPOT[k], i, cc, q] = value[:, :BS]
                    part[1, SPOT[k], i, cc, q] = value[:, BS:]
            return 0

        lax.fori_loop(0, 4, place, 0)
        for c in range(2):
            sib_copies[c, k] = send(part.at[c, SPOT[k], :, 1 - core], sib.at[c, SPOT[k]], dev(dc=1))

    def add(ref, index, *others):
        value = ref[index].astype(F32)
        for other, at in others:
            value = value + other[at].astype(F32)
        return value

    def merge(c, k):
        sib_copies[c, k].wait_recv()
        at = SPOT[k]

        def one(i, _):
            part[c, at, i, core] = part[c, at, i, core] + sib[c, at, i]
            return 0

        lax.fori_loop(0, NY, one, 0)

    def near(value, step, size):
        return rem(value + step + size, size)

    class Reduce:
        def __init__(self, c, half):
            self.c, self.half = c, half
            self.n = c * 2 + half

        def step(self, d):
            return dev(dx=d) if self.half == 0 else dev(dy=d)

        def cross(self, d):
            return dev(dy=d) if self.half == 0 else dev(dx=d)

        def big(self, away, lo, size):
            q = pl.ds(2 * self.half, 2)
            if self.half == 0:
                return (self.c, SPOT[away & 3], pl.ds(lo, size), core, q)
            return (self.c, pl.ds(lo, size), near(y, away, NY), core, q)

        def big_block(self, away, at, q):
            if self.half == 0:
                return (self.c, SPOT[away & 3], at, core, q)
            return (self.c, at, near(y, away, NY), core, 2 + q)

        def small(self, away, q, whole=False):
            if self.half == 0:
                return (self.c, 0, near(y, away, NY), core, q)
            return (self.c, SPOT[away & 3], y, core, pl.ds(2, 2) if whole else 2 + q)

        def far_r(self):
            self.r1 = send(part.at[self.big(2, 0, 2)], land_big1.at[self.n, 0], self.step(1))

        def far_l(self):
            self.l1 = send(part.at[self.big(2, 2, 2)], land_big1.at[self.n, 1], self.step(-1))

        def next_r(self):
            self.r2 = [send(part.at[self.big(1, 2, 2)], land_big2.at[self.n, 0, 2:4], self.step(1))]

        def next_l(self):
            self.l2 = [send(part.at[self.big(-1, 0, 2)], land_big2.at[self.n, 1, 0:2], self.step(-1))]

        def middle(self):
            n = self.n

            def fold(way, lo, away):
                def one(i, _):
                    for q in range(2):
                        at = self.big_block(away, lo + i, q)
                        part[at] = part[at] + land_big1[n, way, i, q]
                    return 0

                lax.fori_loop(0, 2, one, 0)

            self.r1.wait_recv()
            fold(0, 0, 1)
            self.r2.append(send(part.at[self.big(1, 0, 2)], land_big2.at[n, 0, 0:2], self.step(1)))
            self.l1.wait_recv()
            fold(1, 2, -1)
            self.l2.append(send(part.at[self.big(-1, 2, 2)], land_big2.at[n, 1, 2:4], self.step(-1)))

        def turn(self):
            n = self.n
            for copy in self.r2 + self.l2:
                copy.wait_recv()

            def one(i, _):
                for q in range(2):
                    at = self.big_block(0, i, q)
                    part[at] = add(part, at, (land_big2, (n, 0, i, q)), (land_big2, (n, 1, i, q))).astype(BF16)
                return 0

            lax.fori_loop(0, 4, one, 0)
            self.last = [
                send(part.at[self.small(d, pl.ds(0, 2), whole=True)], land_small.at[n, d - 1], self.cross(d))
                for d in (2, 1, 3)
            ]

        def finish(self):
            n = self.n
            for copy in self.last:
                copy.wait_recv()
            for q in range(2):
                value = add(part, self.small(0, q), *[(land_small, (n, d, q)) for d in range(3)])
                row = (2 * self.half + q) * BS
                agg[row:row + BS, self.c * BS:(self.c + 1) * BS] = value.astype(BF16)

    reduces = [[Reduce(c, half) for half in range(2)] for c in range(2)]
    forward(0)
    tile_fa.wait_recv()
    tile_fb.wait_recv()
    forward(2)
    for c in range(2):
        merge(c, 0)
        merge(c, 2)
        reduces[c][1].far_r()
        reduces[c][0].far_r()
        reduces[c][0].far_l()
        reduces[c][1].next_l()
    tile_1.wait_recv()
    forward(1)
    tile_3.wait_recv()
    forward(3)
    for c in range(2):
        merge(c, 1)
        reduces[c][0].next_r()
        merge(c, 3)
        reduces[c][1].far_l()
        reduces[c][1].next_r()
        reduces[c][0].next_l()
    for c in range(2):
        for r in reduces[c]:
            r.middle()
    for k in (2, 1, 3):
        turn(k)
    for stage in ("turn", "finish"):
        for c in range(2):
            for r in reduces[c]:
                getattr(r, stage)()

    pre = jnp.dot(agg[...], weight_ref[...], preferred_element_type=F32)
    gate = jax.nn.sigmoid(pre)
    out_ref[...] = (pre * gate).astype(BF16)
    slope = gate * (1.0 + pre * (1.0 - gate))
    grad_pre = (cot_ref[...].astype(F32) * slope).astype(BF16)
    mixed = lax.dot_general(
        grad_pre, weight_ref[...], (((1,), (1,)), ((), ())), preferred_element_type=F32
    ).astype(BF16)
    for q in range(4):
        for c in range(2):
            grad[c][0, y, core, q] = mixed[q * BS:(q + 1) * BS, c * BS:(c + 1) * BS]

    class Gather:
        def __init__(self, c, half):
            self.c, self.half = c, half
            self.q = pl.ds(2 * half, 2)

        def at(self, first, second, q=None):
            q = self.q if q is None else 2 * self.half + q
            if self.half == 0:
                return (second & 3, near(y, first, NY), core, q)
            return (first & 3, near(y, second, NY), core, q)

        def short(self, d):
            return dev(dy=d) if self.half == 0 else dev(dx=d)

        def long(self, d):
            return dev(dx=d) if self.half == 0 else dev(dy=d)

        def hop(self, first, second, axis, d, q=None):
            there = (first - d, second) if axis == 0 else (first, second - d)
            target = self.short(d) if axis == 0 else self.long(d)
            if self.half == 0:
                there = (first, there[1]) if axis == 1 else (first, second)
            else:
                there = (there[0], second) if axis == 0 else (first, second)
            ref = grad[self.c]
            return send(ref.at[self.at(first, second, q)], ref.at[self.at(*there, q)], target)

        def begin(self):
            self.s = {d: self.hop(0, 0, 0, d) for d in (1, -1, 2)}

        def go(self):
            self.g = {(0, d): self.hop(0, 0, 1, d) for d in (1, -1)}

        def spread(self):
            for d in (1, -1, 2):
                self.s[d].wait_recv()
                for e in (1, -1):
                    self.g[2 if d == 2 else -d, e] = self.hop(-d, 0, 1, e)

        def relay(self):
            self.f = []
            for first in (0, -1):
                self.g[first, 1].wait_recv()
                self.f.append(self.hop(first, -1, 1, 1))
            for first in (1, 2):
                self.g[first, -1].wait_recv()
                self.f.append(self.hop(first, 1, 1, -1))
            self.share(0)

        def share(self, second):
            if self.half == 0:
                at = (second & 3, slice(None), core, self.q)
            else:
                at = (slice(None), near(y, second, NY), core, self.q)
            ref = grad[self.c]
            self.shared.append(send(ref.at[at], ref.at[at], dev(dc=1)))

        def close(self):
            for first in (1, 2):
                self.g[first, 1].wait_recv()
            self.share(-1)
            for first in (0, -1):
                self.g[first, -1].wait_recv()
            self.share(1)

        def close2(self):
            for copy in self.f:
                copy.wait_recv()
            self.share(2)

        def settle(self):
            for copy in self.shared:
                copy.wait_recv()

    gathers = [[Gather(c, half) for half in range(2)] for c in range(2)]
    for pair in gathers:
        for g in pair:
            g.shared = []

    def gather_stage(c, stage):
        for g in gathers[c]:
            getattr(g, stage)()
        if stage == "begin":
            for g in gathers[c]:
                g.go()

    gather_stage(0, "begin")

    w_terms = lax.dot_general(agg[...], grad_pre, (((0,), (0,)), ((), ())), preferred_element_type=F32)
    for p in range(2):
        w_mine[p] = w_terms[p * BS:(p + 1) * BS, :]
    w_copy = send(w_mine.at[1 - core], w_sib, dev(dc=1))
    gather_stage(0, "spread")
    w_copy.wait_recv()
    total = w_mine[core] + w_sib[...]
    for p in range(NZ):
        w_half[p] = total[p * 16:(p + 1) * 16, :].astype(BF16)
    w_z[z] = w_half[z]
    w_copies = [send(w_half.at[near(z, d, NZ)], w_z.at[z], dev(dz=d)) for d in range(1, NZ)]
    gather_stage(1, "begin")
    gather_stage(0, "relay")
    gather_stage(0, "close")
    gather_stage(1, "spread")
    for copy in w_copies:
        copy.wait_recv()
    total = w_z[0].astype(F32)
    for p in range(1, NZ):
        total = total + w_z[p].astype(F32)
    w_x[x] = total
    w_copies = [send(w_x.at[x], w_x.at[x], dev(dx=d)) for d in range(1, NX)]
    gather_stage(0, "close2")
    gather_stage(1, "relay")
    gather_stage(0, "settle")
    for copy in w_copies:
        copy.wait_recv()
    w_y[y] = (w_x[0] + w_x[1]) + (w_x[2] + w_x[3])
    w_copies = [send(w_y.at[y], w_y.at[y], dev(dy=d)) for d in range(1, NY)]

    def backward(c, slot, store):
        for k in range(4):
            m = (slot - lax.div(x + k, jnp.int32(NX))) & 7
            for s in range(2):
                n = k * 2 + s
                at = s * 32 + m * 4 + k
                row, col = meta_s[k, 4, at] & 31, meta_s[k, 5, at]
                tile = turned[k, m, s]
                for q in range(4):
                    lhs[q * BS:(q + 1) * BS, n * BS:(n + 1) * BS] = tile * jnp.where(col == q, 1, 0).astype(BF16)
                rhs[n * BS:(n + 1) * BS, :] = grad[c][k, row >> 3, (row >> 2) & 1, row & 3]
        value = jnp.dot(lhs[...], rhs[...], preferred_element_type=F32)
        for q in range(4):
            store[q] = value[q * BS:(q + 1) * BS, :]

    class Back:
        def __init__(self, c):
            self.c = c

        def put(self, way, t, q, value):
            c = self.c
            z_out[c, way, t, q] = value.astype(BF16)
            self.copies[way, t, q] = send(z_out.at[c, way, t, q], z_in.at[c, way, t, q], dev(dz=1 - 2 * way))

        def begin(self):
            self.copies = {}
            backward(self.c, jnp.int32(4), terms.at[0])
            for q in range(2):
                for way in range(2):
                    self.put(way, 0, 2 * way + q, terms[0, 2 * way + q])

        def step(self, t):
            c = self.c
            away = 4 - t

            def one(way, _):
                backward(c, jnp.where(way == 0, 8 - away, away), terms.at[way])
                return 0

            lax.fori_loop(0, 2, one, 0)
            for q in range(4):
                for way in range(2):
                    at = (q + 2 * (1 - way)) & 3
                    value = terms[way, at]
                    if (way, t - 1, at) in self.copies:
                        self.copies[way, t - 1, at].wait_recv()
                        value = value + z_in[c, way, t - 1, at].astype(F32)
                    self.put(way, t, at, value)

        def finish(self):
            c = self.c
            backward(c, jnp.int32(0), terms.at[0])
            for n in range(4):
                q = (n + 2) & 3
                value = terms[0, q]
                for way in range(2):
                    self.copies[way, 3, q].wait_recv()
                    value = value + z_in[c, way, 3, q].astype(F32)
                gfeat_ref[q * BS:(q + 1) * BS, c * BS:(c + 1) * BS] = value.astype(BF16)

    backs = [Back(0), Back(1)]
    backs[0].begin()
    gather_stage(1, "close")
    for copy in w_copies:
        copy.wait_recv()
    total = (w_y[0] + w_y[1]) + (w_y[2] + w_y[3])
    w_all[core, z] = (total * (1.0 / math.sqrt(NZ * NX * NY * NC * 4 * BS))).astype(BF16)
    w_copies = [send(w_all.at[core, z], w_all.at[core, z], dev(dz=d)) for d in range(1, NZ)]
    backs[0].step(1)
    gather_stage(1, "close2")
    gather_stage(1, "settle")
    backs[1].begin()
    backs[0].step(2)
    backs[1].step(1)
    for copy in w_copies:
        copy.wait_recv()
    w_copy = send(w_all.at[core], w_all.at[core], dev(dc=1))
    backs[0].step(3)
    backs[1].step(2)
    backs[0].finish()
    w_copy.wait_recv()
    for c in range(2):
        for p in range(NZ):
            row = c * BS + p * 16
            gweight_ref[row:row + 16, :] = w_all[c, p].astype(F32)
    backs[1].step(3)
    backs[1].finish()
    for copy in started:
        copy.wait_send()


def hand_over(*refs):
    for source, result in zip(refs[:3], refs[3:]):
        result[...] = source[...]


def body(features, weight, tiles, tile_place, tile_count, cotangent):
    rows, width = features.shape
    tiles = tiles.reshape(8, 4, 2, BS, BS)
    vmem = pl.BlockSpec(memory_space=pltpu.VMEM)
    bf = lambda *lead: pltpu.VMEM(lead + (BS, BS), BF16)
    f32 = lambda *shape: pltpu.VMEM(shape, F32)
    scratch = [
        pltpu.VMEM((8, 4, BS, 2 * BS), BF16),
        bf(8, 2), bf(8, 2), bf(8, 2), bf(8, 2),
        bf(2, 4, 2),
        pltpu.VMEM((4, 8, BS), jnp.int32), pltpu.SMEM((4, 8, BS), jnp.int32),
        pltpu.VMEM((17, BS, 2 * BS), BF16),
        bf(2, 4, 4, 2, 4), bf(2, 4, 4, 4),
        bf(4, 2, 2, 2), bf(4, 2, 4, 2), bf(4, 3, 2),
        pltpu.VMEM((4 * BS, 2 * BS), BF16),
        bf(4, 4, 2, 4), bf(4, 4, 2, 4),
        bf(4, 8, 2),
        pltpu.VMEM((4 * BS, 8 * BS), BF16), pltpu.VMEM((8 * BS, BS), BF16),
        f32(2, 4, BS, BS),
        bf(2, 2, 4, 4), bf(2, 2, 4, 4),
        f32(2, BS, 2 * BS), f32(BS, 2 * BS),
        pltpu.VMEM((8, 16, 2 * BS), BF16), pltpu.VMEM((8, 16, 2 * BS), BF16),
        f32(4, 16, 2 * BS), f32(4, 16, 2 * BS),
        pltpu.VMEM((2, 8, 16, 2 * BS), BF16),
        pltpu.SemaphoreType.DMA((SEM_TOTAL,)), pltpu.SemaphoreType.DMA((SEM_TOTAL,)),
        pltpu.SemaphoreType.DMA, pltpu.SemaphoreType.DMA,
    ]
    shapes = (
        jax.ShapeDtypeStruct((rows, width), BF16),
        jax.ShapeDtypeStruct((rows, width), BF16),
        jax.ShapeDtypeStruct((width, width), F32),
    )
    results = pl.pallas_call(
        kernel,
        out_shape=shapes,
        in_specs=[vmem] * 6,
        out_specs=(vmem,) * 3,
        scratch_shapes=scratch,
        compiler_params=pltpu.CompilerParams(
            collective_id=0, has_side_effects=True, vmem_limit_bytes=56 * 1024 * 1024
        ),
    )(features, weight, tiles, tile_place[0].T, tile_count, cotangent)
    return pl.pallas_call(
        hand_over, out_shape=shapes, in_specs=[vmem] * 3, out_specs=(vmem,) * 3
    )(*results)


def solution(mesh):
    return jax.shard_map(
        body,
        mesh=mesh,
        in_specs=(
            P(("blk", "rep"), None),
            P(),
            P(("blk", "rep"), None, None, None, None),
            P(("blk", "rep"), None, None),
            P(("blk", "rep"), None),
            P(("blk", "rep"), None),
        ),
        out_specs=(P(("blk", "rep"), None), P(("blk", "rep"), None), P()),
        check_vma=False,
    )
```

```python
import functools
import math

import jax
import jax.numpy as jnp
from jax import lax
from jax.experimental import pallas as pl
from jax.experimental.pallas import tpu as pltpu
from jax.sharding import PartitionSpec as P

NZ, NX, NY, NC = 8, 4, 4, 2
BS = 128
F32, BF16 = jnp.float32, jnp.bfloat16
SEM_TOTAL = 320
SPOT = (0, 2, 1, 3)


def rem(a, n):
    return lax.rem(a, jnp.int32(n))


def kernel(
    feat_ref, weight_ref, tiles_ref, place_ref, count_ref, cot_ref,
    out_ref, gfeat_ref, gweight_ref,
    feats, held0, held1, held2, held3, passing, meta, meta_s, sums, part, sib,
    land_big1, land_big2, land_small,
    agg, grad0, grad1, turned, lhs, rhs, terms, z_out, z_in,
    w_mine, w_sib, w_half, w_z, w_x, w_y, w_all,
    send_sem, recv_sem, local_sem, meta_sem,
):
    blk, rep = lax.axis_index("blk"), lax.axis_index("rep")
    z, x = lax.div(blk, jnp.int32(NX)), rem(blk, NX)
    y, core = lax.div(rep, jnp.int32(NC)), rem(rep, NC)

    held, grad = (held0, held1, held2, held3), (grad0, grad1)

    def dev(dz=0, dx=0, dy=0, dc=0):
        return {
            "blk": rem(z + dz + NZ, NZ) * NX + rem(x + dx + NX, NX),
            "rep": rem(y + dy + NY, NY) * NC + rem(core + dc, NC),
        }

    peers = [dev(dc=1)]
    peers += [dev(dx=d) for d in range(1, NX)]
    peers += [dev(dy=d) for d in range(1, NY)]
    peers += [dev(dz=d) for d in range(1, NZ)]
    started = []

    def send(src, dst, target):
        n = len(started)
        copy = pltpu.make_async_remote_copy(
            src_ref=src, dst_ref=dst, send_sem=send_sem.at[n], recv_sem=recv_sem.at[n],
            device_id=target, device_id_type=pl.DeviceIdType.MESH,
        )
        copy.start()
        started.append(copy)
        return copy

    own_tiles = pltpu.make_async_copy(tiles_ref.at[:, 0], held[0], local_sem)
    own_tiles.start()

    barrier = pltpu.get_barrier_semaphore()
    for peer in peers:
        pl.semaphore_signal(barrier, inc=1, device_id=peer, device_id_type=pl.DeviceIdType.MESH)

    for q in range(4):
        feats[0, q] = feat_ref[q * BS:(q + 1) * BS, :]

    pl.semaphore_wait(barrier, len(peers))

    around = {}

    def pass_on(step):
        for half in range(2):
            rows = pl.ds(2 * half, 2)
            for way in (1, -1):
                if step == 3 and half != (way < 0):
                    continue
                if step:
                    around[step - 1, half, way].wait_recv()
                here, there = (way * step) & 7, (way * (step + 1)) & 7
                around[step, half, way] = send(feats.at[here, rows], feats.at[there, rows], dev(dz=way))

    pass_on(0)
    tile_a = send(tiles_ref.at[0:4, 2], passing.at[0], dev(dx=1))
    tile_b = send(tiles_ref.at[4:8, 2], passing.at[1], dev(dx=-1))

    ids = lax.broadcasted_iota(jnp.int32, (BS, BS), 0)
    lanes = lax.broadcasted_iota(jnp.int32, (BS, BS), 1)
    unused = jnp.zeros((1, 64), jnp.int32)
    places = jnp.concatenate([place_ref[0:1, :], place_ref[1:2, :], unused], axis=1)
    counts = jnp.concatenate([count_ref[...], count_ref[...], unused], axis=1)
    places, counts = jnp.broadcast_to(places, (BS, BS)), jnp.broadcast_to(counts, (BS, BS))
    flipped = places + jnp.where(counts > (lanes >> 5), 128, 0)
    code = flipped.T

    def parts_of(value, at):
        inside = at < 64
        live = jnp.logical_and(value >= 128, inside)
        group = jnp.where(inside, at & 3, -1)
        row = jnp.where(live, (value & 127) >> 2, 32)
        return live, group, row, value & 3

    live_e, group_e, row_e, col_e = parts_of(code, ids)
    live_f, group_f, row_f, col_f = parts_of(flipped, lanes)
    key_e, key_f = row_e * 64 + ids, row_f * 64 + lanes
    before = jnp.logical_and(jnp.logical_and(group_e == group_f, lanes < 64), key_f < key_e)

    def count(flags, axis):
        return jnp.sum(jnp.where(flags, 1, 0), axis=axis, keepdims=True)

    rank = count(before, 1)
    same = count(jnp.logical_and(before, row_e == row_f), 1)
    chosen = jnp.logical_and(
        jnp.logical_and(group_e == (lanes >> 4), ids < 64), rank == (lanes & 15)
    )
    entry = ((ids >> 2) & 7) * 2 + (ids >> 5)
    meta[0, 0:1, :] = jnp.sum(jnp.where(chosen, entry, 0), axis=0, keepdims=True)
    meta[0, 1:2, :] = jnp.sum(jnp.where(chosen, col_e, 0), axis=0, keepdims=True)
    meta[0, 2:3, :] = count(jnp.logical_and(chosen, same == 0), 0)
    mine = jnp.logical_and(live_e, group_e == (lanes >> 5))
    here = count(jnp.logical_and(mine, row_e == (lanes & 31)), 0)
    upto = count(jnp.logical_and(mine, row_e <= (lanes & 31)), 0)
    meta[0, 3:4, :] = jnp.where(here > 0, upto - 1, 16)
    meta[0, 4:5, :] = jnp.where(live_f, row_f, 0)[0:1, :]
    meta[0, 5:6, :] = jnp.where(live_f, col_f, 4)[0:1, :]
    meta[0, 6:8, :] = jnp.zeros((2, BS), jnp.int32)
    meta_copies = [send(meta.at[0], meta.at[k], dev(dx=-k)) for k in (1, 2, 3)]
    sums[16] = jnp.zeros((BS, 2 * BS), BF16)

    pass_on(1)
    tile_a.wait_recv()
    tile_fa = send(passing.at[0], held[2].at[0:4], dev(dx=1))
    tile_b.wait_recv()
    tile_fb = send(passing.at[1], held[2].at[4:8], dev(dx=-1))
    tile_1 = send(tiles_ref.at[:, 1], held[1], dev(dx=-1))
    tile_3 = send(tiles_ref.at[:, 3], held[3], dev(dx=1))
    pass_on(2)
    for copy in meta_copies:
        copy.wait_recv()
    to_s = pltpu.make_async_copy(meta, meta_s, meta_sem)
    to_s.start()
    own_tiles.wait()

    def turn(k):
        def one(n, _):
            for s in range(2):
                turned[k, n, s] = held[k][n, s].T
            return 0

        lax.fori_loop(0, 8, one, 0)

    turn(0)
    pass_on(3)
    to_s.wait()
    for key in ((2, 0, -1), (2, 1, 1), (3, 0, 1), (3, 1, -1)):
        around[key].wait_recv()

    sib_copies = {}

    def forward(k):
        carry = lax.div(x + k, jnp.int32(NX))

        def four(g, total):
            for u in range(4):
                at = k * 16 + g * 4 + u
                e, col, fresh = meta_s[k, 0, at] & 15, meta_s[k, 1, at] & 3, meta_s[k, 2, at]
                product = jnp.dot(
                    held[k][e >> 1, e & 1], feats[((e >> 1) + carry) & 7, col], preferred_element_type=F32
                )
                total = product + total * (1 - fresh).astype(F32)
                sums[g * 4 + u] = total.astype(BF16)
            return total

        total = jnp.zeros((BS, 2 * BS), F32)
        for g in range(4):
            total = four(g, total)

        def place(i, _):
            for cc in range(2):
                for q in range(4):
                    row = (i * 2 + cc) * 4 + q
                    value = sums[jnp.clip(meta_s[k, 3, k * 32 + row], 0, 16)]
                    part[0, SPOT[k], i, cc, q] = value[:, :BS]
                    part[1, SPOT[k], i, cc, q] = value[:, BS:]
            return 0

        lax.fori_loop(0, 4, place, 0)
        for c in range(2):
            sib_copies[c, k] = send(part.at[c, SPOT[k], :, 1 - core], sib.at[c, SPOT[k]], dev(dc=1))

    def add(ref, index, *others):
        value = ref[index].astype(F32)
        for other, at in others:
            value = value + other[at].astype(F32)
        return value

    def merge(c, k):
        sib_copies[c, k].wait_recv()
        at = SPOT[k]

        def one(i, _):
            part[c, at, i, core] = part[c, at, i, core] + sib[c, at, i]
            return 0

        lax.fori_loop(0, NY, one, 0)

    def near(value, step, size):
        return rem(value + step + size, size)

    class Reduce:
        def __init__(self, c, half):
            self.c, self.half = c, half
            self.n = c * 2 + half

        def step(self, d):
            return dev(dx=d) if self.half == 0 else dev(dy=d)

        def cross(self, d):
            return dev(dy=d) if self.half == 0 else dev(dx=d)

        def big(self, away, lo, size):
            q = pl.ds(2 * self.half, 2)
            if self.half == 0:
                return (self.c, SPOT[away & 3], pl.ds(lo, size), core, q)
            return (self.c, pl.ds(lo, size), near(y, away, NY), core, q)

        def big_block(self, away, at, q):
            if self.half == 0:
                return (self.c, SPOT[away & 3], at, core, q)
            return (self.c, at, near(y, away, NY), core, 2 + q)

        def small(self, away, q, whole=False):
            if self.half == 0:
                return (self.c, 0, near(y, away, NY), core, q)
            return (self.c, SPOT[away & 3], y, core, pl.ds(2, 2) if whole else 2 + q)

        def far_r(self):
            self.r1 = send(part.at[self.big(2, 0, 2)], land_big1.at[self.n, 0], self.step(1))

        def far_l(self):
            self.l1 = send(part.at[self.big(2, 2, 2)], land_big1.at[self.n, 1], self.step(-1))

        def next_r(self):
            self.r2 = [send(part.at[self.big(1, 2, 2)], land_big2.at[self.n, 0, 2:4], self.step(1))]

        def next_l(self):
            self.l2 = [send(part.at[self.big(-1, 0, 2)], land_big2.at[self.n, 1, 0:2], self.step(-1))]

        def middle(self):
            n = self.n

            def fold(way, lo, away):
                def one(i, _):
                    for q in range(2):
                        at = self.big_block(away, lo + i, q)
                        part[at] = part[at] + land_big1[n, way, i, q]
                    return 0

                lax.fori_loop(0, 2, one, 0)

            self.r1.wait_recv()
            fold(0, 0, 1)
            self.r2.append(send(part.at[self.big(1, 0, 2)], land_big2.at[n, 0, 0:2], self.step(1)))
            self.l1.wait_recv()
            fold(1, 2, -1)
            self.l2.append(send(part.at[self.big(-1, 2, 2)], land_big2.at[n, 1, 2:4], self.step(-1)))

        def turn(self):
            n = self.n
            for copy in self.r2 + self.l2:
                copy.wait_recv()

            def one(i, _):
                for q in range(2):
                    at = self.big_block(0, i, q)
                    part[at] = add(part, at, (land_big2, (n, 0, i, q)), (land_big2, (n, 1, i, q))).astype(BF16)
                return 0

            lax.fori_loop(0, 4, one, 0)
            self.last = [
                send(part.at[self.small(d, pl.ds(0, 2), whole=True)], land_small.at[n, d - 1], self.cross(d))
                for d in (2, 1, 3)
            ]

        def finish(self):
            n = self.n
            for copy in self.last:
                copy.wait_recv()
            for q in range(2):
                value = add(part, self.small(0, q), *[(land_small, (n, d, q)) for d in range(3)])
                row = (2 * self.half + q) * BS
                agg[row:row + BS, self.c * BS:(self.c + 1) * BS] = value.astype(BF16)

    reduces = [[Reduce(c, half) for half in range(2)] for c in range(2)]
    forward(0)
    tile_fa.wait_recv()
    tile_fb.wait_recv()
    forward(2)
    for c in range(2):
        merge(c, 0)
        merge(c, 2)
        reduces[c][1].far_r()
        reduces[c][0].far_r()
        reduces[c][0].far_l()
        reduces[c][1].next_l()
    tile_1.wait_recv()
    forward(1)
    tile_3.wait_recv()
    forward(3)
    for c in range(2):
        merge(c, 1)
        reduces[c][0].next_r()
        merge(c, 3)
        reduces[c][1].far_l()
        reduces[c][1].next_r()
        reduces[c][0].next_l()
    for c in range(2):
        for r in reduces[c]:
            r.middle()
    for k in (2, 1, 3):
        turn(k)
    for stage in ("turn", "finish"):
        for c in range(2):
            for r in reduces[c]:
                getattr(r, stage)()

    pre = jnp.dot(agg[...], weight_ref[...], preferred_element_type=F32)
    gate = jax.nn.sigmoid(pre)
    out_ref[...] = (pre * gate).astype(BF16)
    slope = gate * (1.0 + pre * (1.0 - gate))
    grad_pre = (cot_ref[...].astype(F32) * slope).astype(BF16)
    mixed = lax.dot_general(
        grad_pre, weight_ref[...], (((1,), (1,)), ((), ())), preferred_element_type=F32
    ).astype(BF16)
    for q in range(4):
        for c in range(2):
            grad[c][0, y, core, q] = mixed[q * BS:(q + 1) * BS, c * BS:(c + 1) * BS]

    class Gather:
        def __init__(self, c, half):
            self.c, self.half = c, half
            self.q = pl.ds(2 * half, 2)

        def at(self, first, second, q=None):
            q = self.q if q is None else 2 * self.half + q
            if self.half == 0:
                return (second & 3, near(y, first, NY), core, q)
            return (first & 3, near(y, second, NY), core, q)

        def short(self, d):
            return dev(dy=d) if self.half == 0 else dev(dx=d)

        def long(self, d):
            return dev(dx=d) if self.half == 0 else dev(dy=d)

        def hop(self, first, second, axis, d, q=None):
            there = (first - d, second) if axis == 0 else (first, second - d)
            target = self.short(d) if axis == 0 else self.long(d)
            if self.half == 0:
                there = (first, there[1]) if axis == 1 else (first, second)
            else:
                there = (there[0], second) if axis == 0 else (first, second)
            ref = grad[self.c]
            return send(ref.at[self.at(first, second, q)], ref.at[self.at(*there, q)], target)

        def begin(self):
            self.s = {d: self.hop(0, 0, 0, d) for d in (1, -1, 2)}

        def go(self):
            self.g = {(0, d): self.hop(0, 0, 1, d) for d in (1, -1)}

        def spread(self):
            for d in (1, -1, 2):
                self.s[d].wait_recv()
                for e in (1, -1):
                    self.g[2 if d == 2 else -d, e] = self.hop(-d, 0, 1, e)

        def relay(self):
            self.f = []
            for first in (0, -1):
                self.g[first, 1].wait_recv()
                self.f.append(self.hop(first, -1, 1, 1))
            for first in (1, 2):
                self.g[first, -1].wait_recv()
                self.f.append(self.hop(first, 1, 1, -1))
            self.share(0)

        def share(self, second):
            if self.half == 0:
                at = (second & 3, slice(None), core, self.q)
            else:
                at = (slice(None), near(y, second, NY), core, self.q)
            ref = grad[self.c]
            self.shared.append(send(ref.at[at], ref.at[at], dev(dc=1)))

        def close(self):
            for first in (1, 2):
                self.g[first, 1].wait_recv()
            self.share(-1)
            for first in (0, -1):
                self.g[first, -1].wait_recv()
            self.share(1)

        def close2(self):
            for copy in self.f:
                copy.wait_recv()
            self.share(2)

        def settle(self):
            for copy in self.shared:
                copy.wait_recv()

    gathers = [[Gather(c, half) for half in range(2)] for c in range(2)]
    for pair in gathers:
        for g in pair:
            g.shared = []

    def gather_stage(c, stage):
        for g in gathers[c]:
            getattr(g, stage)()
        if stage == "begin":
            for g in gathers[c]:
                g.go()

    gather_stage(0, "begin")

    w_terms = lax.dot_general(agg[...], grad_pre, (((0,), (0,)), ((), ())), preferred_element_type=F32)
    for p in range(2):
        w_mine[p] = w_terms[p * BS:(p + 1) * BS, :]
    w_copy = send(w_mine.at[1 - core], w_sib, dev(dc=1))
    gather_stage(0, "spread")
    w_copy.wait_recv()
    total = w_mine[core] + w_sib[...]
    for p in range(NZ):
        w_half[p] = total[p * 16:(p + 1) * 16, :].astype(BF16)
    w_z[z] = w_half[z]
    w_copies = [send(w_half.at[near(z, d, NZ)], w_z.at[z], dev(dz=d)) for d in range(1, NZ)]
    gather_stage(1, "begin")
    gather_stage(0, "relay")
    gather_stage(0, "close")
    gather_stage(1, "spread")
    gather_stage(0, "close2")
    gather_stage(1, "relay")
    gather_stage(0, "settle")
    for copy in w_copies:
        copy.wait_recv()
    total = w_z[0].astype(F32)
    for p in range(1, NZ):
        total = total + w_z[p].astype(F32)
    w_x[x] = total
    w_copies = [send(w_x.at[x], w_x.at[x], dev(dx=d)) for d in range(1, NX)]

    def backward(c, slot, store):
        for k in range(4):
            m = (slot - lax.div(x + k, jnp.int32(NX))) & 7
            for s in range(2):
                n = k * 2 + s
                at = s * 32 + m * 4 + k
                row, col = meta_s[k, 4, at] & 31, meta_s[k, 5, at]
                tile = turned[k, m, s]
                for q in range(4):
                    lhs[q * BS:(q + 1) * BS, n * BS:(n + 1) * BS] = tile * jnp.where(col == q, 1, 0).astype(BF16)
                rhs[n * BS:(n + 1) * BS, :] = grad[c][k, row >> 3, (row >> 2) & 1, row & 3]
        value = jnp.dot(lhs[...], rhs[...], preferred_element_type=F32)
        for q in range(4):
            store[q] = value[q * BS:(q + 1) * BS, :]

    class Back:
        def __init__(self, c):
            self.c = c

        def put(self, way, t, q, value):
            c = self.c
            z_out[c, way, t, q] = value.astype(BF16)
            self.copies[way, t, q] = send(z_out.at[c, way, t, q], z_in.at[c, way, t, q], dev(dz=1 - 2 * way))

        def begin(self):
            self.copies = {}
            backward(self.c, jnp.int32(4), terms.at[0])
            for q in range(2):
                for way in range(2):
                    self.put(way, 0, 2 * way + q, terms[0, 2 * way + q])

        def step(self, t):
            c = self.c
            away = 4 - t

            def one(way, _):
                backward(c, jnp.where(way == 0, 8 - away, away), terms.at[way])
                return 0

            lax.fori_loop(0, 2, one, 0)
            for q in range(4):
                for way in range(2):
                    at = (q + 2 * (1 - way)) & 3
                    value = terms[way, at]
                    if (way, t - 1, at) in self.copies:
                        self.copies[way, t - 1, at].wait_recv()
                        value = value + z_in[c, way, t - 1, at].astype(F32)
                    self.put(way, t, at, value)

        def finish(self):
            c = self.c
            backward(c, jnp.int32(0), terms.at[0])
            for n in range(4):
                q = (n + 2) & 3
                value = terms[0, q]
                for way in range(2):
                    self.copies[way, 3, q].wait_recv()
                    value = value + z_in[c, way, 3, q].astype(F32)
                gfeat_ref[q * BS:(q + 1) * BS, c * BS:(c + 1) * BS] = value.astype(BF16)

    backs = [Back(0), Back(1)]
    backs[0].begin()
    gather_stage(1, "close")
    backs[0].step(1)
    gather_stage(1, "close2")
    for copy in w_copies:
        copy.wait_recv()
    w_y[y] = (w_x[0] + w_x[1]) + (w_x[2] + w_x[3])
    w_copies = [send(w_y.at[y], w_y.at[y], dev(dy=d)) for d in range(1, NY)]
    gather_stage(1, "settle")
    backs[1].begin()
    backs[0].step(2)
    for copy in w_copies:
        copy.wait_recv()
    total = (w_y[0] + w_y[1]) + (w_y[2] + w_y[3])
    w_all[core, z] = (total * (1.0 / math.sqrt(NZ * NX * NY * NC * 4 * BS))).astype(BF16)
    w_copies = [send(w_all.at[core, z], w_all.at[core, z], dev(dz=d)) for d in range(1, NZ)]
    backs[1].step(1)
    backs[0].step(3)
    backs[1].step(2)
    for copy in w_copies:
        copy.wait_recv()
    w_copy = send(w_all.at[core], w_all.at[core], dev(dc=1))
    backs[0].finish()
    backs[1].step(3)
    w_copy.wait_recv()
    for c in range(2):
        for p in range(NZ):
            row = c * BS + p * 16
            gweight_ref[row:row + 16, :] = w_all[c, p].astype(F32)
    backs[1].finish()
    for copy in started:
        copy.wait_send()


def hand_over(*refs):
    for source, result in zip(refs[:3], refs[3:]):
        result[...] = source[...]


def body(features, weight, tiles, tile_place, tile_count, cotangent):
    rows, width = features.shape
    tiles = tiles.reshape(8, 4, 2, BS, BS)
    vmem = pl.BlockSpec(memory_space=pltpu.VMEM)
    bf = lambda *lead: pltpu.VMEM(lead + (BS, BS), BF16)
    f32 = lambda *shape: pltpu.VMEM(shape, F32)
    scratch = [
        pltpu.VMEM((8, 4, BS, 2 * BS), BF16),
        bf(8, 2), bf(8, 2), bf(8, 2), bf(8, 2),
        bf(2, 4, 2),
        pltpu.VMEM((4, 8, BS), jnp.int32), pltpu.SMEM((4, 8, BS), jnp.int32),
        pltpu.VMEM((17, BS, 2 * BS), BF16),
        bf(2, 4, 4, 2, 4), bf(2, 4, 4, 4),
        bf(4, 2, 2, 2), bf(4, 2, 4, 2), bf(4, 3, 2),
        pltpu.VMEM((4 * BS, 2 * BS), BF16),
        bf(4, 4, 2, 4), bf(4, 4, 2, 4),
        bf(4, 8, 2),
        pltpu.VMEM((4 * BS, 8 * BS), BF16), pltpu.VMEM((8 * BS, BS), BF16),
        f32(2, 4, BS, BS),
        bf(2, 2, 4, 4), bf(2, 2, 4, 4),
        f32(2, BS, 2 * BS), f32(BS, 2 * BS),
        pltpu.VMEM((8, 16, 2 * BS), BF16), pltpu.VMEM((8, 16, 2 * BS), BF16),
        f32(4, 16, 2 * BS), f32(4, 16, 2 * BS),
        pltpu.VMEM((2, 8, 16, 2 * BS), BF16),
        pltpu.SemaphoreType.DMA((SEM_TOTAL,)), pltpu.SemaphoreType.DMA((SEM_TOTAL,)),
        pltpu.SemaphoreType.DMA, pltpu.SemaphoreType.DMA,
    ]
    shapes = (
        jax.ShapeDtypeStruct((rows, width), BF16),
        jax.ShapeDtypeStruct((rows, width), BF16),
        jax.ShapeDtypeStruct((width, width), F32),
    )
    results = pl.pallas_call(
        kernel,
        out_shape=shapes,
        in_specs=[vmem, vmem, pl.BlockSpec(memory_space=pl.ANY), vmem, vmem, vmem],
        out_specs=(vmem,) * 3,
        scratch_shapes=scratch,
        compiler_params=pltpu.CompilerParams(
            collective_id=0, has_side_effects=True, vmem_limit_bytes=56 * 1024 * 1024
        ),
    )(features, weight, tiles, tile_place[0].T, tile_count, cotangent)
    return pl.pallas_call(
        hand_over, out_shape=shapes, in_specs=[vmem] * 3, out_specs=(vmem,) * 3
    )(*results)


def solution(mesh):
    return jax.shard_map(
        body,
        mesh=mesh,
        in_specs=(
            P(("blk", "rep"), None),
            P(),
            P(("blk", "rep"), None, None, None, None),
            P(("blk", "rep"), None, None),
            P(("blk", "rep"), None),
            P(("blk", "rep"), None),
        ),
        out_specs=(P(("blk", "rep"), None), P(("blk", "rep"), None), P()),
        check_vma=False,
    )
```
